32 devices in a mesh: blk: 8 (over z, core), red: 4 (over y, x).
Axes of the slice: x: 2, y: 2, z: 4, core: 2. Of those that a mesh axis runs over, the one named last changes fastest.
Arguments:
- amplitudes: bfloat16 [8, 192, 128, 128], P(None, 'blk', 'red'), may hold values from -6 to 6
- ladder_ints: bfloat16 [16384, 16384], P('red', 'blk'), may hold values from -0.046875 to 0.046875
- cycle_ints: bfloat16 [24576, 24576], P('blk', 'red'), may hold values from -0.0390625 to 0.0390625
- occ_energy: float32 [192], replicated, may hold values from -2 to -0.3
- vir_energy: float32 [128], replicated, may hold values from 0.2 to 3
- slab_index: int32 [8], replicated, may hold values from 0 to 191
Outputs:
- update: float32 [8, 192, 128, 128], P(None, 'red', 'blk')
The draws below stay inside these ranges and needn't reach their ends.
All inputs are finite; a program needn't handle non-finite values.
Results may differ from the reference program's by a relative error of at most 0.0003.
Values may be sent and summed in bfloat16 or wider, within the bound.
No kernel may reach another device: no remote copies, remote signals or barrier semaphores. Data moves between devices by JAX's collectives and lax.ppermute only.
A program may use at most 192 MiB of HBM per device.

```python
import jax
import jax.numpy as jnp

OCC = 192
VIRT = 128
SLAB = 8


def plant(result, stream_key, low, largest):
    longest = result.shape.index(max(result.shape))
    spots = []
    for shift in (0, 1):
        where = [jax.random.randint(jax.random.fold_in(stream_key, axis), (), 0, length) for axis, length in enumerate(result.shape)]
        where[longest] = (where[longest] + shift) % result.shape[longest]
        spots.append(tuple(where))
    return result.at[spots[0]].set(low).at[spots[1]].set(largest)


def level_of(own_key, extent, pieces, least, top_value):
    level, own = 1.0, jax.random.fold_in(own_key, 6)
    for axis_at, blocks in pieces:
        heights = jnp.exp(jax.random.uniform(jax.random.fold_in(own, axis_at), (blocks,), jnp.float32, least / len(pieces), top_value / len(pieces)))
        level = level * jnp.repeat(heights, extent[axis_at] // blocks).reshape([-1 if axis == axis_at else 1 for axis in range(len(extent))])
    return level


def scatter_about(stream_key, extent, spread, reach, pieces=(), kind=jnp.bfloat16):
    array = jax.random.normal(stream_key, extent, jnp.float32) * spread
    if len(pieces) > 0:
        array = level_of(stream_key, extent, pieces, -0.22, 0.18) * array
    return jnp.clip(array, min=-reach, max=reach).astype(kind)


def setup_inputs(seed: int = 0) -> dict:
    key_list = jax.random.split(jax.random.key(seed), 7)
    amplitudes = scatter_about(key_list[0], (SLAB, OCC, VIRT, VIRT), 1.0, 6.0, ((1, 8), (2, 4)))
    ladder_ints = scatter_about(key_list[1], (VIRT * VIRT, VIRT * VIRT), (VIRT * VIRT) ** -0.5, 0.046875, ((0, 4), (1, 8)))
    cycle_ints = scatter_about(key_list[2], (OCC * VIRT, OCC * VIRT), (OCC * VIRT) ** -0.5, 0.0390625, ((0, 8), (1, 4)))
    occ_energy = jnp.clip(jax.random.uniform(key_list[3], (OCC,), jnp.float32, -2.0, -0.3), -2.0, -0.3)
    vir_energy = jnp.clip(jax.random.uniform(key_list[4], (VIRT,), jnp.float32, 0.2, 3.0), 0.2, 3.0)
    slab_index = plant(jax.random.randint(key_list[5], (SLAB,), 0, OCC), jax.random.fold_in(key_list[5], 1), 0, OCC - 1).astype(jnp.int32)
    return dict(amplitudes=amplitudes, ladder_ints=ladder_ints, cycle_ints=cycle_ints, occ_energy=occ_energy, vir_energy=vir_energy, slab_index=slab_index)


def reference(amplitudes, ladder_ints, cycle_ints, occ_energy, vir_energy, slab_index):
    flattened = amplitudes.reshape(SLAB * OCC, VIRT * VIRT)
    ladder = jnp.dot(flattened, ladder_ints, preferred_element_type=jnp.float32).reshape(SLAB, OCC, VIRT, VIRT)
    operand = jnp.transpose(amplitudes, (0, 2, 1, 3)).reshape(SLAB * VIRT, OCC * VIRT)
    cycle_term = jnp.dot(operand, cycle_ints, preferred_element_type=jnp.float32).reshape(SLAB, VIRT, OCC, VIRT)
    cycle_term = jnp.transpose(cycle_term, (0, 2, 1, 3))
    orbital_ids = jnp.arange(OCC, dtype=jnp.int32)
    chosen = (slab_index.astype(jnp.int32)[:, None] == orbital_ids[None, :])
    slab_energy = jnp.sum(jnp.where(chosen, occ_energy[None, :], jnp.float32(0.0)), axis=1)
    denominator = (vir_energy[None, None, :, None] + vir_energy[None, None, None, :]
                   - slab_energy[:, None, None, None] - occ_energy[None, :, None, None])
    return (ladder + cycle_term) / denominator
```

```python
import functools

import jax
import jax.numpy as jnp
from jax import lax
from jax.experimental import pallas as pl
from jax.experimental.pallas import tpu as pltpu
from jax.sharding import PartitionSpec as P

TRAILER = 16
STEPS = 64.0
TOP = 32000.0
VMEM = 56 * 2**20


def encode(groups):
    rows = lax.broadcasted_iota(jnp.int32, (TRAILER, groups[0].shape[1]), 0)
    trailer = jnp.zeros_like(rows)
    parts = []
    for index, group in enumerate(groups):
        largest = jnp.maximum(jnp.max(jnp.abs(group), axis=0, keepdims=True), 1e-35)
        level = jnp.ceil(jnp.log(largest) * (STEPS / 0.6931471805599453))
        scaled = group * (TOP * jnp.exp2(level * (-1.0 / STEPS)))
        parts.append(jnp.round(scaled).astype(jnp.int32).astype(jnp.int16))
        trailer = jnp.where(rows == index, level.astype(jnp.int32), trailer)
    return parts, trailer.astype(jnp.int16)


def put(ref, groups):
    parts, trailer = encode(groups)
    row = 0
    for part in parts:
        ref[row : row + part.shape[0], :] = part
        row += part.shape[0]
    ref[row : row + TRAILER, :] = trailer


def take(ref, groups, index):
    rows = (ref.shape[0] - TRAILER) // groups
    trailer = ref[groups * rows :, :].astype(jnp.int32).astype(jnp.float32)
    scale = jnp.exp2(trailer[index : index + 1, :] * (1.0 / STEPS)) * (1.0 / TOP)
    return ref[index * rows : (index + 1) * rows, :].astype(jnp.int32).astype(jnp.float32) * scale


def params():
    return pltpu.CompilerParams(vmem_limit_bytes=VMEM, dimension_semantics=("arbitrary",))


def light(flops=1000):
    return pl.CostEstimate(flops=flops, bytes_accessed=1000, transcendentals=0)


def bring(candidates, code, target, sem):
    def start(source):
        return lambda: pltpu.make_async_copy(source, target, sem).start()

    if len(candidates) == 1:
        start(candidates[0])()
    else:
        for number, source in enumerate(candidates):
            pl.when(code == number)(start(source))
    return pltpu.make_async_copy(candidates[0], target, sem)


ANY = pl.BlockSpec(memory_space=pl.ANY)


def forward_kernel(rx_ref, ry_ref, *refs, skip):
    on_y_ref, on_x_ref = refs[skip : skip + 2]
    on_y_ref[...], on_x_ref[...] = rx_ref[...], ry_ref[...]


def forward(rx, ry, through=(), after=()):
    rows, width = rx.shape[0] // 2, rx.shape[1]
    block = jax.ShapeDtypeStruct((rows, width), rx.dtype)
    return pl.pallas_call(
        functools.partial(forward_kernel, skip=len(through) + len(after)),
        grid=(1,),
        in_specs=[pl.BlockSpec((rows, width), lambda n: (0, 0)), pl.BlockSpec((rows, width), lambda n: (1, 0))]
        + [ANY] * (len(through) + len(after)),
        out_specs=[pl.BlockSpec((rows, width), lambda n: (0, 0))] * 2 + [ANY] * len(through),
        out_shape=[block, block] + [jax.ShapeDtypeStruct(t.shape, t.dtype) for t in through],
        input_output_aliases={2 + k: 2 + k for k in range(len(through))},
        compiler_params=params(),
        cost_estimate=light(),
    )(rx, ry, *through, *after)


BLOCKS = 4
SENT = 3


def cycle_kernel(at_ref, own_ref, rx_ref, ry_ref, ry2_ref, rx2_ref, left_ref, right_ref, *refs, keeps, skip):
    if keeps:
        got, refs = refs[:keeps], refs[keeps:]
        sums_ref, s0_ref, s1_ref, s2_ref = refs[skip : 4 + skip]
        x_ref, sems, got_ref = refs[-3:]
        for part, part_ref in enumerate(got):

            @pl.when(pl.program_id(0) // (pl.num_programs(0) // keeps) == part)
            def _(part_ref=part_ref):
                got_ref[...] = part_ref[...]

    else:
        out_ref, x_ref, sems = refs[skip:]
    rows = ry2_ref.shape[0]
    half = at_ref[0]

    @pl.when(pl.program_id(0) == 0)
    def _():
        waits = []
        place = pl.ds(pl.multiple_of(half * rows, rows), rows)
        for n in range(BLOCKS):
            target, sem = x_ref.at[pl.ds(n * rows, rows), :], sems.at[n]
            sources = [own_ref.at[place, :], rx_ref.at[place, :], ry_ref.at[place, :], ry2_ref, rx2_ref]
            code = at_ref[1 + n]
            waits.append(bring(sources, jnp.where(code == 3, 3 + half, code), target, sem))
        for copy in waits:
            copy.wait()

    products = [jnp.dot(x_ref[...], w[...], preferred_element_type=jnp.float32) for w in (left_ref, right_ref)]
    groups = [[p[rows * n : rows * (n + 1)] for p in products] for n in range(BLOCKS)]
    if not keeps:
        put(out_ref, [g for pair in groups for g in pair])
        return
    for n, pair in enumerate(groups):
        totals = [g + take(got_ref, 2 * BLOCKS, 2 * n + side) for side, g in enumerate(pair)]
        for side, total in enumerate(totals):
            sums_ref[n, rows * side : rows * (side + 1), :] = total
        if n < SENT:
            put((s0_ref, s1_ref, s2_ref)[n], totals)


def cycle_call(sources, w, at, part, parts, got=(), after=(), tile=512):
    own, depth = sources[0].shape
    rows, width = own // 2, w.shape[1] // 2
    tiles = width // tile // parts
    first = part * tiles
    operands = [*sources, w, w]
    specs = [ANY] * len(sources) + [
        pl.BlockSpec((depth, tile), lambda n, at: (0, first + n)),
        pl.BlockSpec((depth, tile), lambda n, at: (0, parts * tiles + first + n)),
    ]
    scratch = [pltpu.VMEM((BLOCKS * rows, depth), jnp.bfloat16), pltpu.SemaphoreType.DMA((BLOCKS,))]
    if not got:
        out_shape = jax.ShapeDtypeStruct((2 * BLOCKS * rows + TRAILER, width // parts), jnp.int16)
        out_specs = pl.BlockSpec((2 * BLOCKS * rows + TRAILER, tile), lambda n, at: (0, n))
    else:
        per = tiles // len(got)
        for k, array in enumerate(got):
            operands.append(array)
            shape = (2 * BLOCKS * rows + TRAILER, tile)
            specs.append(pl.BlockSpec(shape, lambda n, at, k=k: (0, jnp.clip(n - k * per, 0, per - 1))))
        scratch.append(pltpu.VMEM((2 * BLOCKS * rows + TRAILER, tile), jnp.int16))
        out_shape = [jax.ShapeDtypeStruct((BLOCKS, own, width), jnp.float32)]
        out_shape += [jax.ShapeDtypeStruct((own + TRAILER, width), jnp.int16)] * SENT
        out_specs = [pl.BlockSpec((BLOCKS, own, tile), lambda n, at: (0, 0, n))]
        out_specs += [pl.BlockSpec((own + TRAILER, tile), lambda n, at: (0, n))] * SENT
    skip = len(after)
    return pl.pallas_call(
        functools.partial(cycle_kernel, keeps=len(got), skip=skip),
        grid_spec=pltpu.PrefetchScalarGridSpec(
            num_scalar_prefetch=1,
            grid=(tiles,),
            in_specs=specs + [ANY] * skip,
            out_specs=out_specs,
            scratch_shapes=scratch,
        ),
        out_shape=out_shape,
        compiler_params=params(),
        cost_estimate=light(),
    )(at, *operands, *after)


def hop_kernel(base_ref, *refs, groups, joins, skip):
    rows = base_ref.shape[1] // groups

    def send(got_ref):
        put(refs[joins + skip], [base_ref[0, rows * g : rows * (g + 1), :] + take(got_ref, groups, g) for g in range(groups)])

    if joins == 1:
        send(refs[0])
    else:
        for part in range(joins):
            pl.when(pl.program_id(0) == part)(functools.partial(send, refs[part]))


def hop(sums, place, got, groups=1, after=(), through=(), parts=2):
    rows, width = sums.shape[1], sums.shape[2]
    tile = width // parts
    got = got if isinstance(got, list) else [got]
    index = (lambda n: (0, n)) if len(got) == 1 else (lambda n: (0, 0))
    skip = len(through) + len(after)
    out = pl.pallas_call(
        functools.partial(hop_kernel, groups=groups, joins=len(got), skip=skip),
        grid=(parts,),
        in_specs=[pl.BlockSpec((1, rows, tile), lambda n: (place, 0, n))]
        + [pl.BlockSpec((rows + TRAILER, tile), index)] * len(got)
        + [ANY] * skip,
        out_specs=[pl.BlockSpec((rows + TRAILER, tile), lambda n: (0, n))] + [ANY] * len(through),
        out_shape=[jax.ShapeDtypeStruct((rows + TRAILER, width), jnp.int16)]
        + [jax.ShapeDtypeStruct(t.shape, t.dtype) for t in through],
        input_output_aliases={1 + len(got) + k: 1 + k for k in range(len(through))},
        compiler_params=params(),
        cost_estimate=light(),
    )(sums, *got, *through, *after)
    return out if through else out[0]


def fill(at_ref, first_code, groups, refs, x_ref, sems):
    @pl.when(pl.program_id(0) == 0)
    def _():
        waits, row, used = [], 0, 0
        for index, count in enumerate(groups):
            rows = refs[used].shape[0]
            target = x_ref.at[pl.ds(row, rows), :]
            waits.append(bring(refs[used : used + count], at_ref[first_code + index], target, sems.at[index]))
            row, used = row + rows, used + count
        for copy in waits:
            copy.wait()


def ladder_one_kernel(at_ref, *refs, groups, after):
    sources, w_ref = refs[: sum(groups)], refs[sum(groups)]
    out_ref, x_ref, sems = refs[sum(groups) + 1 + after :]
    fill(at_ref, 2, groups, sources, x_ref, sems)
    out_ref[...] = jnp.dot(x_ref[...], w_ref[...], preferred_element_type=jnp.float32)


def ladder_pair_kernel(at_ref, *refs, groups, after, prior):
    sources, w_ref = refs[: sum(groups)], refs[sum(groups)]
    prior_ref = refs[sum(groups) + 1]
    keep_ref, message_ref, x_ref, sems, part_ref = refs[sum(groups) + 1 + prior + after :]
    fill(at_ref, 2, groups, sources, x_ref, sems)
    product = jnp.dot(x_ref[...], w_ref[...], preferred_element_type=jnp.float32)
    rows = keep_ref.shape[1]
    if prior:
        part_ref[0] = prior_ref[...]
        part_ref[1] = product
    else:
        part_ref[0] = product[:rows]
        part_ref[1] = product[rows:]
    keep_ref[0] = part_ref[at_ref[1]]
    put(message_ref, [part_ref[1 - at_ref[1]]])


def ladder_call(groups, w, at, pair, prior=None, after=(), columns=1, heavy=False, tile=512):
    depth = groups[0][0].shape[1]
    total = sum(g[0].shape[0] for g in groups)
    width = w.shape[1] // columns
    tiles = width // tile
    counts = tuple(len(g) for g in groups)
    operands = [a for g in groups for a in g] + [w]
    specs = [ANY] * sum(counts) + [pl.BlockSpec((depth, tile), lambda n, at: (0, at[0] * tiles + n))]
    scratch = [pltpu.VMEM((total, depth), jnp.bfloat16), pltpu.SemaphoreType.DMA((len(counts),))]
    if pair:
        rows = total if prior is not None else total // 2
        if prior is not None:
            operands.append(prior)
            specs.append(pl.BlockSpec((rows, tile), lambda n, at: (0, at[0] * tiles + n)))
        kernel = functools.partial(ladder_pair_kernel, groups=counts, after=len(after), prior=int(prior is not None))
        out_shape = [
            jax.ShapeDtypeStruct((1, rows, width), jnp.float32),
            jax.ShapeDtypeStruct((rows + TRAILER, width), jnp.int16),
        ]
        out_specs = [
            pl.BlockSpec((1, rows, tile), lambda n, at: (0, 0, n)),
            pl.BlockSpec((rows + TRAILER, tile), lambda n, at: (0, n)),
        ]
        scratch.append(pltpu.VMEM((2, rows, tile), jnp.float32))
    else:
        kernel = functools.partial(ladder_one_kernel, groups=counts, after=len(after))
        out_shape = jax.ShapeDtypeStruct((total, width), jnp.float32)
        out_specs = pl.BlockSpec((total, tile), lambda n, at: (0, n))
    return pl.pallas_call(
        kernel,
        grid_spec=pltpu.PrefetchScalarGridSpec(
            num_scalar_prefetch=1,
            grid=(tiles,),
            in_specs=specs + [ANY] * len(after),
            out_specs=out_specs,
            scratch_shapes=scratch,
        ),
        out_shape=out_shape,
        compiler_params=params(),
        cost_estimate=light(2 * total * depth * width if heavy else 1000),
    )(at, *operands, *after)


def finish_kernel(at_ref, slab_ref, pair_ref, base_ref, *refs):
    *refs, out_ref, cycle_ref, ladder_ref = refs
    near, core = at_ref[0], at_ref[1]
    refs = list(refs)

    def next_refs(count):
        return [refs.pop(0) for _ in range(count)]

    def scaled(data_ref, trailer_ref, group):
        trailer = trailer_ref[group : group + 1, :].astype(jnp.int32).astype(jnp.float32)
        scale = jnp.exp2(trailer * (1.0 / STEPS)) * (1.0 / TOP)
        return data_ref[...].astype(jnp.int32).astype(jnp.float32) * scale

    base = next_refs(2)
    messages = [next_refs(3) for _ in range(3)]
    for side in range(2):
        cycle_ref[side] = base[side][0] + sum(scaled(m[side], m[2], side) for m in messages)

    block, lanes = out_ref.shape[2:]
    keep0 = next_refs(2)
    chunk0 = [next_refs(3) for _ in range(2)]
    keep1 = next_refs(2)
    chunk1 = [next_refs(3) for _ in range(2)]
    rows = keep0[0].shape[1]

    def spread(keep, chunk):
        for side in range(2):
            total = keep[side][0] + sum(scaled(m[side], m[2], 0) for m in chunk)
            for a in range(block):
                row = (a * 2 + side) * rows
                ladder_ref[row : row + rows, :] = total[:, a * lanes : (a + 1) * lanes]

    pl.when(near == 1)(functools.partial(spread, keep0, chunk0))
    pl.when(near != 1)(functools.partial(spread, keep1, chunk1))

    slab, occ = out_ref.shape[:2]
    per = occ // 2
    step = pl.program_id(0)

    def row(i, carry):
        energy = base_ref[...] - slab_ref[step * slab + i]
        for side in range(2):
            first = jnp.where(core == side, 0, rows)
            for j in range(per):
                ladder = ladder_ref[pl.ds(first + i * per + j, block, stride=2 * rows), :]
                place = pl.ds(pl.multiple_of(i * block, block), block)
                cycle = cycle_ref[side, place, j * lanes : (j + 1) * lanes]
                out_ref[i, side * per + j] = (ladder + cycle) / (energy - pair_ref[side * per + j])
        return carry

    lax.fori_loop(0, slab, row, 0)


def finish(at, slab_energy, pair_energy, base, sums, cycle, chunk0, chunk1, slab, steps=4):
    vir, lanes = base.shape
    occ = pair_energy.shape[0]
    mine, wide = sums.shape[1] // 2 // steps, sums.shape[2]
    operands, specs = [], []

    def add(array, shape, index):
        operands.append(array)
        specs.append(pl.BlockSpec(shape, index))

    def message(array, near=None):
        rows = (array.shape[0] - TRAILER) // 2 // steps
        width = array.shape[1]
        for side in range(2):
            if near is None:
                add(array, (rows, width), lambda n, *_, side=side: (side * steps + n, 0))
            else:
                add(array, (rows, width), lambda n, at, *_, side=side: (jnp.where(at[0] == near, side * steps + n, 0), 0))
        last = (array.shape[0] - TRAILER) // TRAILER
        add(array, (TRAILER, width), lambda n, *_: (last, 0))

    def kept(array, near):
        rows, width = array.shape[1] // 2 // steps, array.shape[2]
        for side in range(2):
            add(array, (1, rows, width), lambda n, at, *_, side=side: (0, jnp.where(at[0] == near, side * steps + n, 0), 0))

    for side in range(2):
        add(sums, (1, mine, wide), lambda n, *_, side=side: (SENT, side * steps + n, 0))
    for array in cycle:
        message(array)
    for near, (keep, *messages) in ((1, chunk0), (0, chunk1)):
        kept(keep, near)
        for array in messages:
            message(array, near)
    rows = chunk0[0].shape[1] // 2 // steps
    return pl.pallas_call(
        finish_kernel,
        grid_spec=pltpu.PrefetchScalarGridSpec(
            num_scalar_prefetch=3,
            grid=(steps,),
            in_specs=[pl.BlockSpec((vir, lanes), lambda n, *_: (0, 0))] + specs,
            out_specs=pl.BlockSpec((slab // steps, occ, vir, lanes), lambda n, *_: (n, 0, 0, 0)),
            scratch_shapes=[
                pltpu.VMEM((2, mine, wide), jnp.float32),
                pltpu.VMEM((2 * vir * rows, lanes), jnp.float32),
            ],
        ),
        out_shape=jax.ShapeDtypeStruct((slab, occ, vir, lanes), jnp.float32),
        compiler_params=params(),
        cost_estimate=light(),
    )(at, slab_energy, pair_energy, base, *operands)


def denominators(occ_energy, vir_energy, slab_index, occ_red, vir_block):
    orbital_ids = jnp.arange(occ_energy.shape[0], dtype=jnp.int32)
    chosen = slab_index[:, None] == orbital_ids[None, :]
    slab_energy = jnp.sum(jnp.where(chosen, occ_energy[None, :], jnp.float32(0.0)), axis=1)
    pair_energy = lax.dynamic_slice_in_dim(occ_energy, lax.axis_index("red") * occ_red, occ_red)
    first_virtual = lax.dynamic_slice_in_dim(vir_energy, lax.axis_index("blk") * vir_block, vir_block)
    return (
        first_virtual[None, None, :, None]
        + vir_energy[None, None, None, :]
        - slab_energy[:, None, None, None]
        - pair_energy[None, :, None, None]
    )


ORDER = ((3, 2, 1, 0), (3, 2, 0, 1), (0, 1, 3, 2), (0, 1, 2, 3))


def paired_shards(amplitudes, ladder_ints, cycle_ints, occ_energy, vir_energy, slab_index):
    slab, occ_local, vir_local, virt = amplitudes.shape
    blk, red = lax.axis_index("blk"), lax.axis_index("red")
    chip, core = blk // 2, blk % 2
    x_place = red % 2
    along_x = [(r, r ^ 1) for r in range(4)]
    along_y = [(r, r ^ 2) for r in range(4)]
    across = [(b, b ^ 1) for b in range(8)]

    def line(*hops):
        return [(2 * a + c, 2 * b + c) for a, b in hops for c in range(2)]

    def trade(pair):
        return lax.all_to_all(pair, "blk", 0, 0, axis_index_groups=[[2 * z, 2 * z + 1] for z in range(4)])

    inward, middle, outward = line((0, 1), (3, 2)), line((1, 2), (2, 1)), line((1, 0), (2, 3))

    def ints(*values):
        return jnp.stack([jnp.asarray(v, jnp.int32) for v in values])

    occ_red, vir_block = 2 * occ_local, vir_local // 2
    zeros = jnp.zeros((8,), jnp.int32)

    mine = amplitudes.reshape(slab, occ_local, 2, vir_block, virt)
    mine = jnp.transpose(mine, (2, 0, 3, 1, 4)).reshape(2 * slab * vir_block, occ_local * virt)
    rx = lax.ppermute(mine, "red", along_x)
    ry = lax.ppermute(mine, "red", along_y)

    own = amplitudes.reshape(slab * occ_local, vir_local * virt)
    g1 = lax.ppermute(own, "blk", line((0, 1), (1, 0), (2, 3), (3, 2)))
    g2 = lax.ppermute(own, "blk", middle)
    own_s = lax.ppermute(own, "blk", across)
    p_own = ladder_call([[own], [own_s]], ladder_ints, zeros, False)

    on_y, on_x, g1, g2 = forward(rx, ry, through=(g1, g2), after=(p_own,))
    rx2 = lax.ppermute(on_x, "red", along_x)
    ry2 = lax.ppermute(on_y, "red", along_y)
    g3 = lax.ppermute(g1, "blk", middle)
    g4 = lax.ppermute(g2, "blk", outward)
    g1_s = lax.ppermute(g1, "blk", across)
    g2_s = lax.ppermute(g2, "blk", across)
    g3_s = lax.ppermute(g3, "blk", across)
    g4_s = lax.ppermute(g4, "blk", across)
    near_x = ints(0, jnp.where(x_place == chip % 2, 0, 1), 0, 0)
    keep0, to_x = ladder_call([[g1], [g1_s]], ladder_ints, near_x, True, prior=p_own)
    x0 = lax.ppermute(to_x, "red", along_x)

    blocks = [mine, rx, ry, ry2, rx2]
    places = jnp.array(ORDER, jnp.int32)[chip] ^ red
    at_give, at_keep = jnp.concatenate([ints(1 - core), places]), jnp.concatenate([ints(core), places])
    give_a = cycle_call(blocks, cycle_ints, at_give, 0, 2, after=(keep0, g2_s))
    got_a = lax.ppermute(give_a, "blk", across)
    give_b = cycle_call(blocks, cycle_ints, at_give, 1, 2, after=(give_a, g3, g4))
    got_b = lax.ppermute(give_b, "blk", across)
    sums, s0, s1, s2 = cycle_call(blocks, cycle_ints, at_keep, 0, 1, [got_a, got_b])
    g5 = lax.ppermute(g3, "blk", outward)
    g5_s = lax.ppermute(g5, "blk", across)
    r0 = lax.ppermute(s0, "blk", inward)
    r1 = lax.ppermute(s1, "blk", inward)
    r2 = lax.ppermute(s2, "blk", inward)

    end = jnp.where((chip == 0) | (chip == 3), 1, 0)
    stays = jnp.where(x_place == chip // 2, 0, 1)
    rest = [[g2, g4], [g2_s, g4_s], [g3, g5], [g3_s, g5_s]]
    keep1, to_x = ladder_call(rest, ladder_ints, ints(0, stays, end, end, end, end), True, after=(sums,))
    x1 = lax.ppermute(to_x, "red", along_x)
    to_mid = hop(sums, 0, r0, 2, after=(keep1,))
    mid = lax.ppermute(to_mid, "blk", middle)
    to_y = hop(keep0, 0, x0, after=(to_mid,))
    y0 = lax.ppermute(to_y, "red", along_y)
    to_inner = hop(sums, 1, r1, 2, after=(to_y,))
    inner = lax.ppermute(to_inner, "blk", middle)
    to_y1 = hop(keep1, 0, x1, after=(to_inner,))
    y1 = lax.ppermute(to_y1, "red", along_y)
    to_outer = hop(sums, 2, mid, 2, after=(to_y1, y0))
    outer = lax.ppermute(to_outer, "blk", outward)

    orbital_ids = jnp.arange(occ_energy.shape[0], dtype=jnp.int32)
    chosen = slab_index[:, None] == orbital_ids[None, :]
    slab_energy = jnp.sum(jnp.where(chosen, occ_energy[None, :], jnp.float32(0.0)), axis=1)
    pair_energy = lax.dynamic_slice_in_dim(occ_energy, red * occ_red, occ_red)
    first_virtual = lax.dynamic_slice_in_dim(vir_energy, blk * vir_block, vir_block)
    base = first_virtual[:, None] + vir_energy[None, :]
    near = jnp.where(red // 2 == chip // 2, 1, 0)
    chunk1 = (keep1, x1, y1)
    cycle = [r2, inner, outer]
    return finish(ints(near, core), slab_energy, pair_energy, base, sums, cycle, (keep0, x0, y0), chunk1, slab)


def plain_shards(amplitudes, ladder_ints, cycle_ints, occ_energy, vir_energy, slab_index):
    slab_rows, occ_local, vir_local, virt_width = amplitudes.shape
    occ_all = occ_local * lax.axis_size("blk")
    occ_red = occ_all // lax.axis_size("red")
    shard_piece = lax.all_gather(amplitudes, "blk", axis=1, tiled=True)
    row_count = shard_piece.shape[1]
    flattened = shard_piece.reshape(slab_rows * row_count, vir_local * virt_width)
    product = jnp.dot(flattened, ladder_ints, preferred_element_type=jnp.float32)
    ladder = product.reshape(slab_rows, row_count, ladder_ints.shape[1])
    ladder_own = lax.psum_scatter(ladder, "red", scatter_dimension=1, tiled=True)
    ladder_own = ladder_own.reshape(slab_rows, occ_red, -1, virt_width)
    shard_piece = lax.all_gather(amplitudes, "red", axis=2, tiled=True)
    vir_count = shard_piece.shape[2]
    operand = jnp.transpose(shard_piece, (0, 2, 1, 3)).reshape(slab_rows * vir_count, occ_local * virt_width)
    product = jnp.dot(operand, cycle_ints, preferred_element_type=jnp.float32)
    cycle_term = product.reshape(slab_rows, vir_count, cycle_ints.shape[1])
    cycle_own = lax.psum_scatter(cycle_term, "blk", scatter_dimension=1, tiled=True)
    vir_block = cycle_own.shape[1]
    cycle_own = jnp.transpose(cycle_own.reshape(slab_rows, vir_block, occ_red, virt_width), (0, 2, 1, 3))
    return (ladder_own + cycle_own) / denominators(occ_energy, vir_energy, slab_index, occ_red, vir_block)


def solution(mesh):
    placed = (P(None, "blk", "red", None), P("red", "blk"), P("blk", "red"), P(), P(), P())
    shards = paired_shards if (mesh.shape["blk"], mesh.shape["red"]) == (8, 4) else plain_shards
    return jax.shard_map(
        shards, mesh=mesh, in_specs=placed, out_specs=P(None, "red", "blk", None), check_vma=False
    )
```

```python
import functools

import jax
import jax.numpy as jnp
from jax import lax
from jax.experimental import pallas as pl
from jax.experimental.pallas import tpu as pltpu
from jax.sharding import PartitionSpec as P

TRAILER = 16
WIDE = 32
STEPS = 64.0
TOP = 32000.0
VMEM = 56 * 2**20


def encode(groups, last):
    rows = lax.broadcasted_iota(jnp.int32, (last, groups[0].shape[1]), 0)
    trailer = jnp.zeros_like(rows)
    parts = []
    for index, group in enumerate(groups):
        largest = jnp.maximum(jnp.max(jnp.abs(group), axis=0, keepdims=True), 1e-35)
        level = jnp.ceil(jnp.log(largest) * (STEPS / 0.6931471805599453))
        scaled = group * (TOP * jnp.exp2(level * (-1.0 / STEPS)))
        parts.append(jnp.round(scaled).astype(jnp.int32).astype(jnp.int16))
        trailer = jnp.where(rows == index, level.astype(jnp.int32), trailer)
    return parts, trailer.astype(jnp.int16)


def put(ref, groups, last=TRAILER):
    parts, trailer = encode(groups, last)
    row = 0
    for part in parts:
        ref[row : row + part.shape[0], :] = part
        row += part.shape[0]
    ref[row : row + last, :] = trailer


def take(ref, groups, index, last=TRAILER):
    rows = (ref.shape[0] - last) // groups
    trailer = ref[groups * rows :, :].astype(jnp.int32).astype(jnp.float32)
    scale = jnp.exp2(trailer[index : index + 1, :] * (1.0 / STEPS)) * (1.0 / TOP)
    return ref[index * rows : (index + 1) * rows, :].astype(jnp.int32).astype(jnp.float32) * scale


def params():
    return pltpu.CompilerParams(vmem_limit_bytes=VMEM, dimension_semantics=("arbitrary",))


def light(weight=0):
    return pl.CostEstimate(flops=weight * 1150000000 + 1000, bytes_accessed=1000, transcendentals=0)


def bring(candidates, code, target, sem):
    def start(source):
        return lambda: pltpu.make_async_copy(source, target, sem).start()

    if len(candidates) == 1:
        start(candidates[0])()
    else:
        for number, source in enumerate(candidates):
            pl.when(code == number)(start(source))
    return pltpu.make_async_copy(candidates[0], target, sem)


ANY = pl.BlockSpec(memory_space=pl.ANY)


def forward_kernel(rx_ref, ry_ref, *refs, skip):
    on_y_ref, on_x_ref = refs[skip : skip + 2]
    on_y_ref[...], on_x_ref[...] = rx_ref[...], ry_ref[...]


def forward(rx, ry, through=(), after=()):
    rows, width = rx.shape[0] // 2, rx.shape[1]
    block = jax.ShapeDtypeStruct((rows, width), rx.dtype)
    return pl.pallas_call(
        functools.partial(forward_kernel, skip=len(through) + len(after)),
        grid=(1,),
        in_specs=[pl.BlockSpec((rows, width), lambda n: (0, 0)), pl.BlockSpec((rows, width), lambda n: (1, 0))]
        + [ANY] * (len(through) + len(after)),
        out_specs=[pl.BlockSpec((rows, width), lambda n: (0, 0))] * 2 + [ANY] * len(through),
        out_shape=[block, block] + [jax.ShapeDtypeStruct(t.shape, t.dtype) for t in through],
        input_output_aliases={2 + k: 2 + k for k in range(len(through))},
        compiler_params=params(),
        cost_estimate=light(),
    )(rx, ry, *through, *after)


BLOCKS = 4
SENT = 3
PARTS = 2


def cycle_kernel(at_ref, own_ref, rx_ref, ry_ref, ry2_ref, rx2_ref, left_ref, right_ref, *refs, keeps, skip):
    if keeps:
        got_ref = refs[0]
        sums_ref, s0_ref, s1_ref, s2_ref, x_ref, sems = refs[1 + skip :]
    else:
        out_ref, x_ref, sems = refs[skip:]
    rows = ry2_ref.shape[0]
    half = at_ref[0]

    @pl.when(pl.program_id(0) == 0)
    def _():
        waits = []
        place = pl.ds(pl.multiple_of(half * rows, rows), rows)
        for n in range(BLOCKS):
            target, sem = x_ref.at[pl.ds(n * rows, rows), :], sems.at[n]
            sources = [own_ref.at[place, :], rx_ref.at[place, :], ry_ref.at[place, :], ry2_ref, rx2_ref]
            code = at_ref[1 + n]
            waits.append(bring(sources, jnp.where(code == 3, 3 + half, code), target, sem))
        for copy in waits:
            copy.wait()

    products = [jnp.dot(x_ref[...], w[...], preferred_element_type=jnp.float32) for w in (left_ref, right_ref)]
    groups = [[p[rows * n : rows * (n + 1)] for p in products] for n in range(BLOCKS)]
    if not keeps:
        put(out_ref, [g for pair in groups for g in pair])
        return
    for n, pair in enumerate(groups):
        totals = [g + take(got_ref, 2 * BLOCKS, 2 * n + side) for side, g in enumerate(pair)]
        for side, total in enumerate(totals):
            sums_ref[n, rows * side : rows * (side + 1), :] = total
        if n < SENT:
            put((s0_ref, s1_ref, s2_ref)[n], totals)


def cycle_call(sources, w, at, part, got=None, before=(), after=(), tile=512):
    own, depth = sources[0].shape
    rows, width = own // 2, w.shape[1] // 2
    tiles = width // tile // PARTS
    first = part * tiles
    operands = [*sources, w, w]
    specs = [ANY] * len(sources) + [
        pl.BlockSpec((depth, tile), lambda n, at: (0, first + n)),
        pl.BlockSpec((depth, tile), lambda n, at: (0, PARTS * tiles + first + n)),
    ]
    given = pl.BlockSpec((2 * BLOCKS * rows + TRAILER, tile), lambda n, at: (0, n))
    aliases = {}
    if got is None:
        out_shape = jax.ShapeDtypeStruct((2 * BLOCKS * rows + TRAILER, width // PARTS), jnp.int16)
        out_specs = given
    else:
        operands.append(got)
        specs.append(given)
        if before:
            aliases = {1 + len(operands): 0, 2 + len(operands): 2, 3 + len(operands): 3}
        message = jax.ShapeDtypeStruct((own + TRAILER, width), jnp.int16)
        out_shape = [
            jax.ShapeDtypeStruct((BLOCKS, own, width), jnp.float32),
            jax.ShapeDtypeStruct((own + TRAILER, width // PARTS), jnp.int16),
            message,
            message,
        ]
        out_specs = [
            pl.BlockSpec((BLOCKS, own, tile), lambda n, at: (0, 0, first + n)),
            pl.BlockSpec((own + TRAILER, tile), lambda n, at: (0, n)),
        ] + [pl.BlockSpec((own + TRAILER, tile), lambda n, at: (0, first + n))] * 2
    skip = len(before) + len(after)
    return pl.pallas_call(
        functools.partial(cycle_kernel, keeps=got is not None, skip=skip),
        grid_spec=pltpu.PrefetchScalarGridSpec(
            num_scalar_prefetch=1,
            grid=(tiles,),
            in_specs=specs + [ANY] * skip,
            out_specs=out_specs,
            scratch_shapes=[pltpu.VMEM((BLOCKS * rows, depth), jnp.bfloat16), pltpu.SemaphoreType.DMA((BLOCKS,))],
        ),
        out_shape=out_shape,
        input_output_aliases=aliases,
        compiler_params=params(),
        cost_estimate=light(19),
    )(at, *operands, *before, *after)


def hop_kernel(base_ref, *refs, joins, skip, trailer):
    rows = base_ref.shape[1] // 2

    def send(got_ref):
        put(refs[joins + skip], [base_ref[0, rows * g : rows * (g + 1), :] + take(got_ref, 2, g) for g in range(2)], trailer)

    if joins == 1:
        send(refs[0])
    else:
        for part in range(joins):
            pl.when(pl.program_id(0) == part)(functools.partial(send, refs[part]))


def hop(sums, place, got, part=0, parts=1, through=(), after=(), weight=4, trailer=TRAILER):
    rows, tile = sums.shape[1], sums.shape[2] // 2
    joins = len(got)
    skip = len(through) + len(after)
    index = (lambda n: (0, n)) if joins == 1 else (lambda n: (0, 0))
    out = pl.pallas_call(
        functools.partial(hop_kernel, joins=joins, skip=skip, trailer=trailer),
        grid=(parts,),
        in_specs=[pl.BlockSpec((1, rows, tile), lambda n: (place, 0, part + n))]
        + [pl.BlockSpec((rows + TRAILER, tile), index)] * joins
        + [ANY] * skip,
        out_specs=[pl.BlockSpec((rows + trailer, tile), lambda n: (0, n))] + [ANY] * len(through),
        out_shape=[jax.ShapeDtypeStruct((rows + trailer, parts * tile), jnp.int16)]
        + [jax.ShapeDtypeStruct(t.shape, t.dtype) for t in through],
        input_output_aliases={1 + joins + k: 1 + k for k in range(len(through))},
        compiler_params=params(),
        cost_estimate=light(weight),
    )(sums, *got, *through, *after)
    return out if through else out[0]


def fill(at_ref, first_code, groups, refs, x_ref, sems):
    @pl.when(pl.program_id(0) == 0)
    def _():
        waits, row, used = [], 0, 0
        for index, count in enumerate(groups):
            rows = refs[used].shape[0]
            target = x_ref.at[pl.ds(row, rows), :]
            waits.append(bring(refs[used : used + count], at_ref[first_code + index], target, sems.at[index]))
            row, used = row + rows, used + count
        for copy in waits:
            copy.wait()


def ladder_one_kernel(at_ref, *refs, groups, after):
    sources, w_ref = refs[: sum(groups)], refs[sum(groups)]
    out_ref, x_ref, sems = refs[sum(groups) + 1 + after :]
    fill(at_ref, 2, groups, sources, x_ref, sems)
    out_ref[...] = jnp.dot(x_ref[...], w_ref[...], preferred_element_type=jnp.float32)


def ladder_pair_kernel(at_ref, *refs, groups, after, prior, trailer):
    sources, w_ref = refs[: sum(groups)], refs[sum(groups)]
    prior_ref = refs[sum(groups) + 1]
    keep_ref, message_ref, x_ref, sems, part_ref = refs[sum(groups) + 1 + prior + after :]
    fill(at_ref, 2, groups, sources, x_ref, sems)
    product = jnp.dot(x_ref[...], w_ref[...], preferred_element_type=jnp.float32)
    rows = keep_ref.shape[1]
    if prior:
        part_ref[0] = prior_ref[...]
        part_ref[1] = product
    else:
        part_ref[0] = product[:rows]
        part_ref[1] = product[rows:]
    keep_ref[0] = part_ref[at_ref[1]]
    put(message_ref, [part_ref[1 - at_ref[1]]], trailer)


def ladder_call(groups, w, at, pair, prior=None, after=(), columns=1, trailer=TRAILER, tile=512):
    depth = groups[0][0].shape[1]
    total = sum(g[0].shape[0] for g in groups)
    width = w.shape[1] // columns
    tiles = width // tile
    counts = tuple(len(g) for g in groups)
    operands = [a for g in groups for a in g] + [w]
    specs = [ANY] * sum(counts) + [pl.BlockSpec((depth, tile), lambda n, at: (0, at[0] * tiles + n))]
    scratch = [pltpu.VMEM((total, depth), jnp.bfloat16), pltpu.SemaphoreType.DMA((len(counts),))]
    if pair:
        rows = total if prior is not None else total // 2
        if prior is not None:
            operands.append(prior)
            specs.append(pl.BlockSpec((rows, tile), lambda n, at: (0, at[0] * tiles + n)))
        kernel = functools.partial(ladder_pair_kernel, groups=counts, after=len(after), prior=int(prior is not None), trailer=trailer)
        out_shape = [
            jax.ShapeDtypeStruct((1, rows, width), jnp.float32),
            jax.ShapeDtypeStruct((rows + trailer, width), jnp.int16),
        ]
        out_specs = [
            pl.BlockSpec((1, rows, tile), lambda n, at: (0, 0, n)),
            pl.BlockSpec((rows + trailer, tile), lambda n, at: (0, n)),
        ]
        scratch.append(pltpu.VMEM((2, rows, tile), jnp.float32))
    else:
        kernel = functools.partial(ladder_one_kernel, groups=counts, after=len(after))
        out_shape = jax.ShapeDtypeStruct((total, width), jnp.float32)
        out_specs = pl.BlockSpec((total, tile), lambda n, at: (0, n))
    return pl.pallas_call(
        kernel,
        grid_spec=pltpu.PrefetchScalarGridSpec(
            num_scalar_prefetch=1,
            grid=(tiles,),
            in_specs=specs + [ANY] * len(after),
            out_specs=out_specs,
            scratch_shapes=scratch,
        ),
        out_shape=out_shape,
        compiler_params=params(),
        cost_estimate=light(),
    )(at, *operands, *after)


def turn_kernel(at_ref, *refs, trailer):
    for near, (base_ref, got_ref) in enumerate((refs[2:4], refs[0:2])):

        @pl.when(at_ref[0] == near)
        def _(near=near, base_ref=base_ref, got_ref=got_ref):
            put(refs[-1], [base_ref[0] + take(got_ref, 1, 0, WIDE if near else TRAILER)], trailer)


def turn(at, chunk0, chunk1, part, after=(), weight=4, trailer=TRAILER):
    _, rows, width = chunk1[0].shape
    operands, specs = [], []
    for (keep, got), index in ((chunk0, part), (chunk1, 0)):
        operands += [keep, got]
        specs.append(pl.BlockSpec((1, rows, width), lambda n, at, index=index: (0, 0, index)))
        specs.append(pl.BlockSpec((got.shape[0], width), lambda n, at, index=index: (0, index)))
    return pl.pallas_call(
        functools.partial(turn_kernel, trailer=trailer),
        grid_spec=pltpu.PrefetchScalarGridSpec(
            num_scalar_prefetch=1,
            grid=(1,),
            in_specs=specs + [ANY] * len(after),
            out_specs=pl.BlockSpec((rows + trailer, width), lambda n, at: (0, n)),
        ),
        out_shape=jax.ShapeDtypeStruct((rows + trailer, width), jnp.int16),
        compiler_params=params(),
        cost_estimate=light(weight),
    )(at, *operands, *after)


def finish_kernel(at_ref, slab_ref, pair_ref, base_ref, *refs):
    *refs, out_ref, cycle_ref, ladder_ref = refs
    near, core = at_ref[0], at_ref[1]
    refs = list(refs)

    def next_refs(count):
        return [refs.pop(0) for _ in range(count)]

    def scaled(data_ref, trailer_ref, group):
        trailer = trailer_ref[group : group + 1, :].astype(jnp.int32).astype(jnp.float32)
        scale = jnp.exp2(trailer * (1.0 / STEPS)) * (1.0 / TOP)
        return data_ref[...].astype(jnp.int32).astype(jnp.float32) * scale

    base = next_refs(2)
    messages = [next_refs(3) for _ in range(3)]
    for side in range(2):
        cycle_ref[side] = base[side][0] + sum(scaled(m[side], m[2], side) for m in messages)

    block, lanes = out_ref.shape[2:]
    keep0, x0 = next_refs(2), next_refs(3)
    chunk1 = [(next_refs(2), next_refs(3)) for _ in range(2)]
    came = [next_refs(3) for _ in range(2)]
    rows = keep0[0].shape[1]

    def spread(part, side, total):
        total = total + scaled(came[part][side], came[part][2], 0)
        for a in range(block // 2):
            row = ((part * (block // 2) + a) * 2 + side) * rows
            ladder_ref[row : row + rows, :] = total[:, a * lanes : (a + 1) * lanes]

    @pl.when(near == 1)
    def _():
        for side in range(2):
            total = keep0[side][0] + scaled(x0[side], x0[2], 0)
            half = total.shape[1] // 2
            for part in range(2):
                spread(part, side, total[:, part * half : (part + 1) * half])

    @pl.when(near != 1)
    def _():
        for part, (keep, got) in enumerate(chunk1):
            for side in range(2):
                spread(part, side, keep[side][0] + scaled(got[side], got[2], 0))

    slab, occ = out_ref.shape[:2]
    per = occ // 2
    step = pl.program_id(0)

    def row(i, carry):
        energy = base_ref[...] - slab_ref[step * slab + i]
        for side in range(2):
            first = jnp.where(core == side, 0, rows)
            for j in range(per):
                ladder = ladder_ref[pl.ds(first + i * per + j, block, stride=2 * rows), :]
                place = pl.ds(pl.multiple_of(i * block, block), block)
                cycle = cycle_ref[side, place, j * lanes : (j + 1) * lanes]
                out_ref[i, side * per + j] = (ladder + cycle) / (energy - pair_ref[side * per + j])
        return carry

    lax.fori_loop(0, slab, row, 0)


def finish(at, slab_energy, pair_energy, base, sums, cycle, chunk0, chunk1, came, slab, steps=4):
    vir, lanes = base.shape
    occ = pair_energy.shape[0]
    mine, wide = sums.shape[1] // 2 // steps, sums.shape[2]
    operands, specs = [], []

    def add(array, shape, index):
        operands.append(array)
        specs.append(pl.BlockSpec(shape, index))

    def message(array, trailer, near=None):
        rows = (array.shape[0] - trailer) // 2 // steps
        width = array.shape[1]
        for side in range(2):
            if near is None:
                add(array, (rows, width), lambda n, *_, side=side: (side * steps + n, 0))
            else:
                add(array, (rows, width), lambda n, at, *_, side=side: (jnp.where(at[0] == near, side * steps + n, 0), 0))
        last = (array.shape[0] - trailer) // trailer
        add(array, (trailer, width), lambda n, *_: (last, 0))

    def kept(array, near):
        rows, width = array.shape[1] // 2 // steps, array.shape[2]
        for side in range(2):
            add(array, (1, rows, width), lambda n, at, *_, side=side: (0, jnp.where(at[0] == near, side * steps + n, 0), 0))

    for side in range(2):
        add(sums, (1, mine, wide), lambda n, *_, side=side: (SENT, side * steps + n, 0))
    for array in cycle:
        message(array, array.shape[0] - sums.shape[1])
    kept(chunk0[0], 1)
    message(chunk0[1], WIDE, 1)
    for keep, got in chunk1:
        kept(keep, 0)
        message(got, TRAILER, 0)
    for array in came:
        message(array, array.shape[0] - chunk0[0].shape[1])
    rows = chunk0[0].shape[1] // 2 // steps
    return pl.pallas_call(
        finish_kernel,
        grid_spec=pltpu.PrefetchScalarGridSpec(
            num_scalar_prefetch=3,
            grid=(steps,),
            in_specs=[pl.BlockSpec((vir, lanes), lambda n, *_: (0, 0))] + specs,
            out_specs=pl.BlockSpec((slab // steps, occ, vir, lanes), lambda n, *_: (n, 0, 0, 0)),
            scratch_shapes=[
                pltpu.VMEM((2, mine, wide), jnp.float32),
                pltpu.VMEM((2 * vir * rows, lanes), jnp.float32),
            ],
        ),
        out_shape=jax.ShapeDtypeStruct((slab, occ, vir, lanes), jnp.float32),
        compiler_params=params(),
        cost_estimate=light(),
    )(at, slab_energy, pair_energy, base, *operands)


def denominators(occ_energy, vir_energy, slab_index, occ_red, vir_block):
    orbital_ids = jnp.arange(occ_energy.shape[0], dtype=jnp.int32)
    chosen = slab_index[:, None] == orbital_ids[None, :]
    slab_energy = jnp.sum(jnp.where(chosen, occ_energy[None, :], jnp.float32(0.0)), axis=1)
    pair_energy = lax.dynamic_slice_in_dim(occ_energy, lax.axis_index("red") * occ_red, occ_red)
    first_virtual = lax.dynamic_slice_in_dim(vir_energy, lax.axis_index("blk") * vir_block, vir_block)
    return (
        first_virtual[None, None, :, None]
        + vir_energy[None, None, None, :]
        - slab_energy[:, None, None, None]
        - pair_energy[None, :, None, None]
    )


ORDER = ((3, 2, 1, 0), (3, 2, 0, 1), (0, 1, 3, 2), (0, 1, 2, 3))


def paired_shards(amplitudes, ladder_ints, cycle_ints, occ_energy, vir_energy, slab_index):
    slab, occ_local, vir_local, virt = amplitudes.shape
    blk, red = lax.axis_index("blk"), lax.axis_index("red")
    chip, core = blk // 2, blk % 2
    x_place = red % 2
    along_x = [(r, r ^ 1) for r in range(4)]
    along_y = [(r, r ^ 2) for r in range(4)]
    across = [(b, b ^ 1) for b in range(8)]

    def line(*hops):
        return [(2 * a + c, 2 * b + c) for a, b in hops for c in range(2)]

    def trade(pair):
        return lax.all_to_all(pair, "blk", 0, 0, axis_index_groups=[[2 * z, 2 * z + 1] for z in range(4)])

    inward, middle, outward = line((0, 1), (3, 2)), line((1, 2), (2, 1)), line((1, 0), (2, 3))

    def ints(*values):
        return jnp.stack([jnp.asarray(v, jnp.int32) for v in values])

    occ_red, vir_block = 2 * occ_local, vir_local // 2
    zeros = jnp.zeros((8,), jnp.int32)

    mine = amplitudes.reshape(slab, occ_local, 2, vir_block, virt)
    mine = jnp.transpose(mine, (2, 0, 3, 1, 4)).reshape(2 * slab * vir_block, occ_local * virt)
    rx = lax.ppermute(mine, "red", along_x)
    ry = lax.ppermute(mine, "red", along_y)

    own = amplitudes.reshape(slab * occ_local, vir_local * virt)
    g1 = lax.ppermute(own, "blk", line((0, 1), (1, 0), (2, 3), (3, 2)))
    g2 = lax.ppermute(own, "blk", middle)
    own_s = lax.ppermute(own, "blk", across)
    p_own = ladder_call([[own], [own_s]], ladder_ints, zeros, False)

    on_y, on_x, g1, g2 = forward(rx, ry, through=(g1, g2), after=(p_own,))
    rx2 = lax.ppermute(on_x, "red", along_x)
    ry2 = lax.ppermute(on_y, "red", along_y)
    g3 = lax.ppermute(g1, "blk", middle)
    g4 = lax.ppermute(g2, "blk", outward)
    g1_s = lax.ppermute(g1, "blk", across)
    g2_s = lax.ppermute(g2, "blk", across)
    g3_s = lax.ppermute(g3, "blk", across)
    g4_s = lax.ppermute(g4, "blk", across)
    near_x = ints(0, jnp.where(x_place == chip % 2, 0, 1), 0, 0)
    keep0, to_x = ladder_call([[g1], [g1_s]], ladder_ints, near_x, True, prior=p_own, trailer=WIDE)
    x0 = lax.ppermute(to_x, "red", along_x)

    blocks = [mine, rx, ry, ry2, rx2]
    places = jnp.array(ORDER, jnp.int32)[chip] ^ red
    at_give, at_keep = jnp.concatenate([ints(1 - core), places]), jnp.concatenate([ints(core), places])
    give_a = cycle_call(blocks, cycle_ints, at_give, 0, after=(keep0, g2_s))
    got_a = lax.ppermute(give_a, "blk", across)
    give_b = cycle_call(blocks, cycle_ints, at_give, 1, after=(give_a, g3, g4))
    got_b = lax.ppermute(give_b, "blk", across)
    sums, s0a, s1, s2 = cycle_call(blocks, cycle_ints, at_keep, 0, got_a, after=(give_b,))
    r0a = lax.ppermute(s0a, "blk", inward)
    sums, s0b, s1, s2 = cycle_call(blocks, cycle_ints, at_keep, 1, got_b, (sums, s1, s2))
    r0b = lax.ppermute(s0b, "blk", inward)
    g5 = lax.ppermute(g3, "blk", outward)

    to_mid, s1, s2, g5 = hop(sums, 0, [r0a], 0, through=(s1, s2, g5))
    g5_s = lax.ppermute(g5, "blk", across)
    mid_a = lax.ppermute(to_mid, "blk", middle)
    r1 = lax.ppermute(s1, "blk", inward)
    end = jnp.where((chip == 0) | (chip == 3), 1, 0)
    stays = jnp.where(x_place == chip // 2, 0, 1)
    rest = [[g2, g4], [g2_s, g4_s], [g3, g5], [g3_s, g5_s]]
    at = ints(0, stays, end, end, end, end)
    keep1, to_x = ladder_call(rest, ladder_ints, at, True, after=(to_mid, x0), columns=2)
    x1 = lax.ppermute(to_x, "red", along_x)
    to_mid = hop(sums, 0, [r0b], 1, after=(keep1,))
    mid_b = lax.ppermute(to_mid, "blk", middle)
    at = ints(1, stays, end, end, end, end)
    keep2, to_x = ladder_call(rest, ladder_ints, at, True, after=(to_mid,), columns=2)
    x2 = lax.ppermute(to_x, "red", along_x)
    to_outer = hop(sums, 2, [mid_a, mid_b], parts=2, after=(keep2,), weight=0, trailer=WIDE)
    outer = lax.ppermute(to_outer, "blk", outward)
    near = jnp.where(red // 2 == chip // 2, 1, 0)
    to_y1 = turn(ints(1 - near), (keep0, x0), (keep1, x1), 0, after=(to_outer,), weight=0, trailer=WIDE)
    y1 = lax.ppermute(to_y1, "red", along_y)
    to_inner, s2 = hop(sums, 1, [r1], parts=2, through=(s2,), after=(to_y1,), weight=8)
    r2 = lax.ppermute(s2, "blk", inward)
    inner = lax.ppermute(to_inner, "blk", middle)
    to_y2 = turn(ints(1 - near), (keep0, x0), (keep2, x2), 1, after=(to_inner,), weight=4)
    y2 = lax.ppermute(to_y2, "red", along_y)

    orbital_ids = jnp.arange(occ_energy.shape[0], dtype=jnp.int32)
    chosen = slab_index[:, None] == orbital_ids[None, :]
    slab_energy = jnp.sum(jnp.where(chosen, occ_energy[None, :], jnp.float32(0.0)), axis=1)
    pair_energy = lax.dynamic_slice_in_dim(occ_energy, red * occ_red, occ_red)
    first_virtual = lax.dynamic_slice_in_dim(vir_energy, blk * vir_block, vir_block)
    base = first_virtual[:, None] + vir_energy[None, :]
    cycle = [r2, inner, outer]
    at = ints(near, core)
    chunk1 = [(keep1, x1), (keep2, x2)]
    return finish(at, slab_energy, pair_energy, base, sums, cycle, (keep0, x0), chunk1, [y1, y2], slab)


def plain_shards(amplitudes, ladder_ints, cycle_ints, occ_energy, vir_energy, slab_index):
    slab_rows, occ_local, vir_local, virt_width = amplitudes.shape
    occ_all = occ_local * lax.axis_size("blk")
    occ_red = occ_all // lax.axis_size("red")
    shard_piece = lax.all_gather(amplitudes, "blk", axis=1, tiled=True)
    row_count = shard_piece.shape[1]
    flattened = shard_piece.reshape(slab_rows * row_count, vir_local * virt_width)
    product = jnp.dot(flattened, ladder_ints, preferred_element_type=jnp.float32)
    ladder = product.reshape(slab_rows, row_count, ladder_ints.shape[1])
    ladder_own = lax.psum_scatter(ladder, "red", scatter_dimension=1, tiled=True)
    ladder_own = ladder_own.reshape(slab_rows, occ_red, -1, virt_width)
    shard_piece = lax.all_gather(amplitudes, "red", axis=2, tiled=True)
    vir_count = shard_piece.shape[2]
    operand = jnp.transpose(shard_piece, (0, 2, 1, 3)).reshape(slab_rows * vir_count, occ_local * virt_width)
    product = jnp.dot(operand, cycle_ints, preferred_element_type=jnp.float32)
    cycle_term = product.reshape(slab_rows, vir_count, cycle_ints.shape[1])
    cycle_own = lax.psum_scatter(cycle_term, "blk", scatter_dimension=1, tiled=True)
    vir_block = cycle_own.shape[1]
    cycle_own = jnp.transpose(cycle_own.reshape(slab_rows, vir_block, occ_red, virt_width), (0, 2, 1, 3))
    return (ladder_own + cycle_own) / denominators(occ_energy, vir_energy, slab_index, occ_red, vir_block)


def solution(mesh):
    placed = (P(None, "blk", "red", None), P("red", "blk"), P("blk", "red"), P(), P(), P())
    shards = paired_shards if (mesh.shape["blk"], mesh.shape["red"]) == (8, 4) else plain_shards
    return jax.shard_map(
        shards, mesh=mesh, in_specs=placed, out_specs=P(None, "red", "blk", None), check_vma=False
    )
```

```python
import functools

import jax
import jax.numpy as jnp
from jax import lax
from jax.experimental import pallas as pl
from jax.experimental.pallas import tpu as pltpu
from jax.sharding import PartitionSpec as P

TRAILER = 16
WIDE = 32
STEPS = 64.0
TOP = 32000.0
VMEM = 56 * 2**20


def encode(groups, last):
    rows = lax.broadcasted_iota(jnp.int32, (last, groups[0].shape[1]), 0)
    trailer = jnp.zeros_like(rows)
    parts = []
    for index, group in enumerate(groups):
        largest = jnp.maximum(jnp.max(jnp.abs(group), axis=0, keepdims=True), 1e-35)
        level = jnp.ceil(jnp.log(largest) * (STEPS / 0.6931471805599453))
        scaled = group * (TOP * jnp.exp2(level * (-1.0 / STEPS)))
        parts.append(jnp.round(scaled).astype(jnp.int32).astype(jnp.int16))
        trailer = jnp.where(rows == index, level.astype(jnp.int32), trailer)
    return parts, trailer.astype(jnp.int16)


def put(ref, groups, last=TRAILER):
    parts, trailer = encode(groups, last)
    row = 0
    for part in parts:
        ref[row : row + part.shape[0], :] = part
        row += part.shape[0]
    ref[row : row + last, :] = trailer


def take(ref, groups, index, last=TRAILER):
    rows = (ref.shape[0] - last) // groups
    trailer = ref[groups * rows :, :].astype(jnp.int32).astype(jnp.float32)
    scale = jnp.exp2(trailer[index : index + 1, :] * (1.0 / STEPS)) * (1.0 / TOP)
    return ref[index * rows : (index + 1) * rows, :].astype(jnp.int32).astype(jnp.float32) * scale


def params():
    return pltpu.CompilerParams(vmem_limit_bytes=VMEM, dimension_semantics=("arbitrary",))


def light(weight=0):
    return pl.CostEstimate(flops=weight * 1150000000 + 1000, bytes_accessed=1000, transcendentals=0)


def bring(candidates, code, target, sem):
    def start(source):
        return lambda: pltpu.make_async_copy(source, target, sem).start()

    if len(candidates) == 1:
        start(candidates[0])()
    else:
        for number, source in enumerate(candidates):
            pl.when(code == number)(start(source))
    return pltpu.make_async_copy(candidates[0], target, sem)


ANY = pl.BlockSpec(memory_space=pl.ANY)


def forward_kernel(rx_ref, ry_ref, *refs, skip):
    on_y_ref, on_x_ref, sems = refs[skip], refs[skip + 1], refs[-1]
    rows = on_y_ref.shape[0]
    copies = [
        pltpu.make_async_copy(rx_ref.at[pl.ds(0, rows), :], on_y_ref, sems.at[0]),
        pltpu.make_async_copy(ry_ref.at[pl.ds(rows, rows), :], on_x_ref, sems.at[1]),
    ]
    for copy in copies:
        copy.start()
    for copy in copies:
        copy.wait()


def forward(rx, ry, through=(), after=()):
    rows, width = rx.shape[0] // 2, rx.shape[1]
    block = jax.ShapeDtypeStruct((rows, width), rx.dtype)
    return pl.pallas_call(
        functools.partial(forward_kernel, skip=len(through) + len(after)),
        grid=(1,),
        in_specs=[ANY] * (2 + len(through) + len(after)),
        out_specs=[pl.BlockSpec((rows, width), lambda n: (0, 0))] * 2 + [ANY] * len(through),
        scratch_shapes=[pltpu.SemaphoreType.DMA((2,))],
        out_shape=[block, block] + [jax.ShapeDtypeStruct(t.shape, t.dtype) for t in through],
        input_output_aliases={2 + k: 2 + k for k in range(len(through))},
        compiler_params=params(),
        cost_estimate=light(),
    )(rx, ry, *through, *after)


BLOCKS = 4
SENT = 3
PARTS = 2


def cycle_kernel(at_ref, own_ref, rx_ref, ry_ref, ry2_ref, rx2_ref, left_ref, right_ref, *refs, keeps, skip):
    if keeps:
        got_ref = refs[0]
        sums_ref, s0_ref, s1_ref, s2_ref, x_ref, sems = refs[1 + skip :]
    else:
        out_ref, x_ref, sems = refs[skip:]
    rows = ry2_ref.shape[0]
    half = at_ref[0]

    @pl.when(pl.program_id(0) == 0)
    def _():
        waits = []
        place = pl.ds(pl.multiple_of(half * rows, rows), rows)
        for n in range(BLOCKS):
            target, sem = x_ref.at[pl.ds(n * rows, rows), :], sems.at[n]
            sources = [own_ref.at[place, :], rx_ref.at[place, :], ry_ref.at[place, :], ry2_ref, rx2_ref]
            code = at_ref[1 + n]
            waits.append(bring(sources, jnp.where(code == 3, 3 + half, code), target, sem))
        for copy in waits:
            copy.wait()

    products = [jnp.dot(x_ref[...], w[...], preferred_element_type=jnp.float32) for w in (left_ref, right_ref)]
    groups = [[p[rows * n : rows * (n + 1)] for p in products] for n in range(BLOCKS)]
    if not keeps:
        put(out_ref, [g for pair in groups for g in pair])
        return
    for n, pair in enumerate(groups):
        totals = [g + take(got_ref, 2 * BLOCKS, 2 * n + side) for side, g in enumerate(pair)]
        for side, total in enumerate(totals):
            sums_ref[n, rows * side : rows * (side + 1), :] = total
        if n < SENT:
            put((s0_ref, s1_ref, s2_ref)[n], totals, WIDE if n == SENT - 1 else TRAILER)


def cycle_call(sources, w, at, part, got=None, before=(), after=(), tile=256):
    own, depth = sources[0].shape
    rows, width = own // 2, w.shape[1] // 2
    tiles = width // tile // PARTS
    first = part * tiles
    operands = [*sources, w, w]
    specs = [ANY] * len(sources) + [
        pl.BlockSpec((depth, tile), lambda n, at: (0, first + n)),
        pl.BlockSpec((depth, tile), lambda n, at: (0, PARTS * tiles + first + n)),
    ]
    given = pl.BlockSpec((2 * BLOCKS * rows + TRAILER, tile), lambda n, at: (0, n))
    aliases = {}
    if got is None:
        out_shape = jax.ShapeDtypeStruct((2 * BLOCKS * rows + TRAILER, width // PARTS), jnp.int16)
        out_specs = given
    else:
        operands.append(got)
        specs.append(given)
        if before:
            aliases = {1 + len(operands): 0, 2 + len(operands): 2, 3 + len(operands): 3}
        out_shape = [
            jax.ShapeDtypeStruct((BLOCKS, own, width), jnp.float32),
            jax.ShapeDtypeStruct((own + TRAILER, width // PARTS), jnp.int16),
            jax.ShapeDtypeStruct((own + TRAILER, width), jnp.int16),
            jax.ShapeDtypeStruct((own + WIDE, width), jnp.int16),
        ]
        out_specs = [
            pl.BlockSpec((BLOCKS, own, tile), lambda n, at: (0, 0, first + n)),
            pl.BlockSpec((own + TRAILER, tile), lambda n, at: (0, n)),
            pl.BlockSpec((own + TRAILER, tile), lambda n, at: (0, first + n)),
            pl.BlockSpec((own + WIDE, tile), lambda n, at: (0, first + n)),
        ]
    skip = len(before) + len(after)
    return pl.pallas_call(
        functools.partial(cycle_kernel, keeps=got is not None, skip=skip),
        grid_spec=pltpu.PrefetchScalarGridSpec(
            num_scalar_prefetch=1,
            grid=(tiles,),
            in_specs=specs + [ANY] * skip,
            out_specs=out_specs,
            scratch_shapes=[pltpu.VMEM((BLOCKS * rows, depth), jnp.bfloat16), pltpu.SemaphoreType.DMA((BLOCKS,))],
        ),
        out_shape=out_shape,
        input_output_aliases=aliases,
        compiler_params=params(),
        cost_estimate=light(19),
    )(at, *operands, *before, *after)


def gate_kernel(*refs):
    refs[-1][...] = jnp.zeros_like(refs[-1])


def gate(*through, after=()):
    out = pl.pallas_call(
        gate_kernel,
        in_specs=[ANY] * (len(through) + len(after)),
        out_specs=[ANY] * len(through) + [pl.BlockSpec(memory_space=pltpu.VMEM)],
        out_shape=[jax.ShapeDtypeStruct(t.shape, t.dtype) for t in through] + [jax.ShapeDtypeStruct((8, 128), jnp.float32)],
        input_output_aliases={k: k for k in range(len(through))},
        cost_estimate=light(),
    )(*through, *after)
    return out[:-1]


def hop_kernel(base_ref, *refs, joins, skip, trailer):
    rows = base_ref.shape[1] // 2

    def send(got_ref):
        put(refs[joins + skip], [base_ref[0, rows * g : rows * (g + 1), :] + take(got_ref, 2, g) for g in range(2)], trailer)

    if joins == 1:
        send(refs[0])
    else:
        for part in range(joins):
            pl.when(pl.program_id(0) == part)(functools.partial(send, refs[part]))


def hop(sums, place, got, part=0, parts=1, through=(), after=(), weight=4, trailer=TRAILER):
    rows, tile = sums.shape[1], sums.shape[2] // 2
    joins = len(got)
    skip = len(through) + len(after)
    index = (lambda n: (0, n)) if joins == 1 else (lambda n: (0, 0))
    out = pl.pallas_call(
        functools.partial(hop_kernel, joins=joins, skip=skip, trailer=trailer),
        grid=(parts,),
        in_specs=[pl.BlockSpec((1, rows, tile), lambda n: (place, 0, part + n))]
        + [pl.BlockSpec((rows + TRAILER, tile), index)] * joins
        + [ANY] * skip,
        out_specs=[pl.BlockSpec((rows + trailer, tile), lambda n: (0, n))] + [ANY] * len(through),
        out_shape=[jax.ShapeDtypeStruct((rows + trailer, parts * tile), jnp.int16)]
        + [jax.ShapeDtypeStruct(t.shape, t.dtype) for t in through],
        input_output_aliases={1 + joins + k: 1 + k for k in range(len(through))},
        compiler_params=params(),
        cost_estimate=light(weight),
    )(sums, *got, *through, *after)
    return out if through else out[0]


def fill(at_ref, first_code, groups, refs, x_ref, sems):
    @pl.when(pl.program_id(0) == 0)
    def _():
        waits, row, used = [], 0, 0
        for index, count in enumerate(groups):
            rows = refs[used].shape[0]
            target = x_ref.at[pl.ds(row, rows), :]
            waits.append(bring(refs[used : used + count], at_ref[first_code + index], target, sems.at[index]))
            row, used = row + rows, used + count
        for copy in waits:
            copy.wait()


def ladder_one_kernel(at_ref, *refs, groups, after):
    sources, w_ref = refs[: sum(groups)], refs[sum(groups)]
    out_ref, x_ref, sems = refs[sum(groups) + 1 + after :]
    fill(at_ref, 2, groups, sources, x_ref, sems)
    out_ref[...] = jnp.dot(x_ref[...], w_ref[...], preferred_element_type=jnp.float32)


def ladder_pair_kernel(at_ref, *refs, groups, after, prior, trailer):
    sources, w_ref = refs[: sum(groups)], refs[sum(groups)]
    prior_ref = refs[sum(groups) + 1]
    keep_ref, message_ref, x_ref, sems, part_ref = refs[sum(groups) + 1 + prior + after :]
    fill(at_ref, 2, groups, sources, x_ref, sems)
    product = jnp.dot(x_ref[...], w_ref[...], preferred_element_type=jnp.float32)
    rows = keep_ref.shape[1]
    if prior:
        part_ref[0] = prior_ref[...]
        part_ref[1] = product
    else:
        part_ref[0] = product[:rows]
        part_ref[1] = product[rows:]
    keep_ref[0] = part_ref[at_ref[1]]
    put(message_ref, [part_ref[1 - at_ref[1]]], trailer)


def ladder_call(groups, w, at, pair, prior=None, after=(), columns=1, trailer=TRAILER, tile=512):
    depth = groups[0][0].shape[1]
    total = sum(g[0].shape[0] for g in groups)
    width = w.shape[1] // columns
    tiles = width // tile
    counts = tuple(len(g) for g in groups)
    operands = [a for g in groups for a in g] + [w]
    specs = [ANY] * sum(counts) + [pl.BlockSpec((depth, tile), lambda n, at: (0, at[0] * tiles + n))]
    scratch = [pltpu.VMEM((total, depth), jnp.bfloat16), pltpu.SemaphoreType.DMA((len(counts),))]
    if pair:
        rows = total if prior is not None else total // 2
        if prior is not None:
            operands.append(prior)
            specs.append(pl.BlockSpec((rows, tile), lambda n, at: (0, at[0] * tiles + n)))
        kernel = functools.partial(ladder_pair_kernel, groups=counts, after=len(after), prior=int(prior is not None), trailer=trailer)
        out_shape = [
            jax.ShapeDtypeStruct((1, rows, width), jnp.float32),
            jax.ShapeDtypeStruct((rows + trailer, width), jnp.int16),
        ]
        out_specs = [
            pl.BlockSpec((1, rows, tile), lambda n, at: (0, 0, n)),
            pl.BlockSpec((rows + trailer, tile), lambda n, at: (0, n)),
        ]
        scratch.append(pltpu.VMEM((2, rows, tile), jnp.float32))
    else:
        kernel = functools.partial(ladder_one_kernel, groups=counts, after=len(after))
        out_shape = jax.ShapeDtypeStruct((total, width), jnp.float32)
        out_specs = pl.BlockSpec((total, tile), lambda n, at: (0, n))
    return pl.pallas_call(
        kernel,
        grid_spec=pltpu.PrefetchScalarGridSpec(
            num_scalar_prefetch=1,
            grid=(tiles,),
            in_specs=specs + [ANY] * len(after),
            out_specs=out_specs,
            scratch_shapes=scratch,
        ),
        out_shape=out_shape,
        compiler_params=params(),
        cost_estimate=light(),
    )(at, *operands, *after)


def turn_kernel(at_ref, *refs, trailer):
    for near, (base_ref, got_ref) in enumerate((refs[2:4], refs[0:2])):

        @pl.when(at_ref[0] == near)
        def _(near=near, base_ref=base_ref, got_ref=got_ref):
            put(refs[-1], [base_ref[0] + take(got_ref, 1, 0, WIDE if near else TRAILER)], trailer)


def turn(at, chunk0, chunk1, part, after=(), weight=4, trailer=TRAILER):
    _, rows, width = chunk1[0].shape
    operands, specs = [], []
    for (keep, got), index in ((chunk0, part), (chunk1, 0)):
        operands += [keep, got]
        specs.append(pl.BlockSpec((1, rows, width), lambda n, at, index=index: (0, 0, index)))
        specs.append(pl.BlockSpec((got.shape[0], width), lambda n, at, index=index: (0, index)))
    return pl.pallas_call(
        functools.partial(turn_kernel, trailer=trailer),
        grid_spec=pltpu.PrefetchScalarGridSpec(
            num_scalar_prefetch=1,
            grid=(1,),
            in_specs=specs + [ANY] * len(after),
            out_specs=pl.BlockSpec((rows + trailer, width), lambda n, at: (0, n)),
        ),
        out_shape=jax.ShapeDtypeStruct((rows + trailer, width), jnp.int16),
        compiler_params=params(),
        cost_estimate=light(weight),
    )(at, *operands, *after)


def scaled(message, side, group):
    trailer = message[2][group : group + 1, :].astype(jnp.int32).astype(jnp.float32)
    scale = jnp.exp2(trailer * (1.0 / STEPS)) * (1.0 / TOP)
    return message[side][...].astype(jnp.int32).astype(jnp.float32) * scale


class Blocks:
    def __init__(self, steps):
        self.steps, self.operands, self.specs = steps, [], []

    def add(self, array, shape, index):
        self.operands.append(array)
        self.specs.append(pl.BlockSpec(shape, index))

    def place(self, at, side, n, near):
        place = side * self.steps + n
        return place if near is None else jnp.where(at[0] == near, place, 0)

    def message(self, array, trailer, near=None):
        rows, width = (array.shape[0] - trailer) // 2 // self.steps, array.shape[1]
        for side in range(2):
            self.add(array, (rows, width), lambda n, at, *_, side=side: (self.place(at, side, n, near), 0))
        last = (array.shape[0] - trailer) // trailer
        self.add(array, (trailer, width), lambda n, *_: (last, 0))

    def sides(self, array, first, near=None):
        rows, width = array.shape[1] // 2 // self.steps, array.shape[2]
        for side in range(2):
            self.add(array, (1, rows, width), lambda n, at, *_, side=side: (first, self.place(at, side, n, near), 0))


def settle_kernel(at_ref, *refs):
    *refs, out_ref, cycle_ref, ladder_ref = refs
    near, core = at_ref[0], at_ref[1]
    refs = list(refs)

    def next_refs(count):
        return [refs.pop(0) for _ in range(count)]

    base, chain = next_refs(2), next_refs(3)
    for side in range(2):
        cycle_ref[side] = base[side][0] + scaled(chain, side, side)

    slab, occ, block, lanes = out_ref.shape
    keep0, x0 = next_refs(2), next_refs(3)
    chunk1 = [(next_refs(2), next_refs(3)) for _ in range(2)]
    came = [next_refs(3) for _ in range(2)]
    rows = keep0[0].shape[1]

    def spread(part, side, total):
        total = total + scaled(came[part], side, 0)
        for a in range(block // 2):
            row = ((part * (block // 2) + a) * 2 + side) * rows
            ladder_ref[row : row + rows, :] = total[:, a * lanes : (a + 1) * lanes]

    @pl.when(near == 1)
    def _():
        for side in range(2):
            total = keep0[side][0] + scaled(x0, side, 0)
            half = total.shape[1] // 2
            for part in range(2):
                spread(part, side, total[:, part * half : (part + 1) * half])

    @pl.when(near != 1)
    def _():
        for part, (keep, got) in enumerate(chunk1):
            for side in range(2):
                spread(part, side, keep[side][0] + scaled(got, side, 0))

    per = occ // 2

    def row(i, carry):
        for side in range(2):
            first = jnp.where(core == side, 0, rows)
            for j in range(per):
                ladder = ladder_ref[pl.ds(first + i * per + j, block, stride=2 * rows), :]
                place = pl.ds(pl.multiple_of(i * block, block), block)
                out_ref[i, side * per + j] = ladder + cycle_ref[side, place, j * lanes : (j + 1) * lanes]
        return carry

    lax.fori_loop(0, slab, row, 0)


def settle(at, shape, sums, outer, chunk0, chunk1, came, steps=4):
    slab, occ, vir, lanes = shape
    mine, wide = sums.shape[1] // 2 // steps, sums.shape[2]
    blocks = Blocks(steps)
    blocks.sides(sums, SENT)
    blocks.message(outer, WIDE)
    blocks.sides(chunk0[0], 0, 1)
    blocks.message(chunk0[1], WIDE, 1)
    for keep, got in chunk1:
        blocks.sides(keep, 0, 0)
        blocks.message(got, TRAILER, 0)
    for array in came:
        blocks.message(array, array.shape[0] - chunk0[0].shape[1])
    rows = chunk0[0].shape[1] // 2 // steps
    return pl.pallas_call(
        settle_kernel,
        grid_spec=pltpu.PrefetchScalarGridSpec(
            num_scalar_prefetch=1,
            grid=(steps,),
            in_specs=blocks.specs,
            out_specs=pl.BlockSpec((slab // steps, occ, vir, lanes), lambda n, *_: (n, 0, 0, 0)),
            scratch_shapes=[
                pltpu.VMEM((2, mine, wide), jnp.float32),
                pltpu.VMEM((2 * vir * rows, lanes), jnp.float32),
            ],
        ),
        out_shape=jax.ShapeDtypeStruct(shape, jnp.float32),
        compiler_params=params(),
        cost_estimate=light(7),
    )(at, *blocks.operands)


def finish_kernel(at_ref, slab_ref, pair_ref, base_ref, settled_ref, *refs):
    first, second = refs[0:3], refs[3:6]
    out_ref, cycle_ref = refs[6:]
    for side in range(2):
        cycle_ref[side] = scaled(first, side, side) + scaled(second, side, side)
    slab, occ, block, lanes = out_ref.shape
    per = occ // 2
    step = pl.program_id(0)

    def row(i, carry):
        energy = base_ref[...] - slab_ref[step * slab + i]
        place = pl.ds(pl.multiple_of(i * block, block), block)
        for side in range(2):
            for j in range(per):
                total = settled_ref[i, side * per + j] + cycle_ref[side, place, j * lanes : (j + 1) * lanes]
                out_ref[i, side * per + j] = total / (energy - pair_ref[side * per + j])
        return carry

    lax.fori_loop(0, slab, row, 0)


def finish(at, slab_energy, pair_energy, base, settled, cycle, steps=2):
    slab, occ, vir, lanes = settled.shape
    blocks = Blocks(steps)
    blocks.add(base, base.shape, lambda n, *_: (0, 0))
    blocks.add(settled, (slab // steps, occ, vir, lanes), lambda n, *_: (n, 0, 0, 0))
    for array, trailer in zip(cycle, (WIDE, TRAILER)):
        blocks.message(array, trailer)
    wide = cycle[0].shape[1]
    return pl.pallas_call(
        finish_kernel,
        grid_spec=pltpu.PrefetchScalarGridSpec(
            num_scalar_prefetch=3,
            grid=(steps,),
            in_specs=blocks.specs,
            out_specs=pl.BlockSpec((slab // steps, occ, vir, lanes), lambda n, *_: (n, 0, 0, 0)),
            scratch_shapes=[pltpu.VMEM((2, slab * vir // steps, wide), jnp.float32)],
        ),
        out_shape=jax.ShapeDtypeStruct(settled.shape, jnp.float32),
        compiler_params=params(),
        cost_estimate=light(),
    )(at, slab_energy, pair_energy, *blocks.operands)


def denominators(occ_energy, vir_energy, slab_index, occ_red, vir_block):
    orbital_ids = jnp.arange(occ_energy.shape[0], dtype=jnp.int32)
    chosen = slab_index[:, None] == orbital_ids[None, :]
    slab_energy = jnp.sum(jnp.where(chosen, occ_energy[None, :], jnp.float32(0.0)), axis=1)
    pair_energy = lax.dynamic_slice_in_dim(occ_energy, lax.axis_index("red") * occ_red, occ_red)
    first_virtual = lax.dynamic_slice_in_dim(vir_energy, lax.axis_index("blk") * vir_block, vir_block)
    return (
        first_virtual[None, None, :, None]
        + vir_energy[None, None, None, :]
        - slab_energy[:, None, None, None]
        - pair_energy[None, :, None, None]
    )


ORDER = ((3, 2, 1, 0), (3, 2, 0, 1), (0, 1, 3, 2), (0, 1, 2, 3))


def paired_shards(amplitudes, ladder_ints, cycle_ints, occ_energy, vir_energy, slab_index):
    slab, occ_local, vir_local, virt = amplitudes.shape
    blk, red = lax.axis_index("blk"), lax.axis_index("red")
    chip, core = blk // 2, blk % 2
    x_place = red % 2
    along_x = [(r, r ^ 1) for r in range(4)]
    along_y = [(r, r ^ 2) for r in range(4)]
    across = [(b, b ^ 1) for b in range(8)]

    def line(*hops):
        return [(2 * a + c, 2 * b + c) for a, b in hops for c in range(2)]

    def trade(pair):
        return lax.all_to_all(pair, "blk", 0, 0, axis_index_groups=[[2 * z, 2 * z + 1] for z in range(4)])

    inward, middle, outward = line((0, 1), (3, 2)), line((1, 2), (2, 1)), line((1, 0), (2, 3))

    def ints(*values):
        return jnp.stack([jnp.asarray(v, jnp.int32) for v in values])

    occ_red, vir_block = 2 * occ_local, vir_local // 2
    zeros = jnp.zeros((8,), jnp.int32)

    mine = amplitudes.reshape(slab, occ_local, 2, vir_block, virt)
    mine = jnp.transpose(mine, (2, 0, 3, 1, 4)).reshape(2 * slab * vir_block, occ_local * virt)
    rx = lax.ppermute(mine, "red", along_x)
    ry = lax.ppermute(mine, "red", along_y)

    own = amplitudes.reshape(slab * occ_local, vir_local * virt)
    g1 = lax.ppermute(own, "blk", line((0, 1), (1, 0), (2, 3), (3, 2)))
    g2 = lax.ppermute(own, "blk", middle)
    own_s = lax.ppermute(own, "blk", across)
    p_own = ladder_call([[own], [own_s]], ladder_ints, zeros, False)

    on_y, on_x, g1, g2 = forward(rx, ry, through=(g1, g2), after=(p_own,))
    rx2 = lax.ppermute(on_x, "red", along_x)
    ry2 = lax.ppermute(on_y, "red", along_y)
    g3 = lax.ppermute(g1, "blk", middle)
    g4 = lax.ppermute(g2, "blk", outward)
    g1_s = lax.ppermute(g1, "blk", across)
    g2_s = lax.ppermute(g2, "blk", across)
    g3_s = lax.ppermute(g3, "blk", across)
    g4_s = lax.ppermute(g4, "blk", across)
    near_x = ints(0, jnp.where(x_place == chip % 2, 0, 1), 0, 0)
    keep0, to_x = ladder_call([[g1], [g1_s]], ladder_ints, near_x, True, prior=p_own, trailer=WIDE)
    x0 = lax.ppermute(to_x, "red", along_x)

    blocks = [mine, rx, ry, ry2, rx2]
    places = jnp.array(ORDER, jnp.int32)[chip] ^ red
    at_give, at_keep = jnp.concatenate([ints(1 - core), places]), jnp.concatenate([ints(core), places])
    give_a = cycle_call(blocks, cycle_ints, at_give, 0, after=(keep0, g2_s))
    got_a = lax.ppermute(give_a, "blk", across)
    give_b = cycle_call(blocks, cycle_ints, at_give, 1, after=(give_a, g3, g4))
    got_b = lax.ppermute(give_b, "blk", across)
    sums, s0a, s1, s2 = cycle_call(blocks, cycle_ints, at_keep, 0, got_a, after=(give_b,))
    r0a = lax.ppermute(s0a, "blk", inward)
    sums, s0b, s1, s2 = cycle_call(blocks, cycle_ints, at_keep, 1, got_b, (sums, s1, s2))
    r0b = lax.ppermute(s0b, "blk", inward)
    g5 = lax.ppermute(g3, "blk", outward)

    s1, s2, g5 = gate(s1, s2, g5, after=(sums, r0a))
    to_mid = hop(sums, 0, [r0a], 0, after=(s1,))
    g5_s = lax.ppermute(g5, "blk", across)
    mid_a = lax.ppermute(to_mid, "blk", middle)
    r1 = lax.ppermute(s1, "blk", inward)
    end = jnp.where((chip == 0) | (chip == 3), 1, 0)
    stays = jnp.where(x_place == chip // 2, 0, 1)
    rest = [[g2, g4], [g2_s, g4_s], [g3, g5], [g3_s, g5_s]]
    at = ints(0, stays, end, end, end, end)
    keep1, to_x = ladder_call(rest, ladder_ints, at, True, after=(to_mid, x0), columns=2)
    x1 = lax.ppermute(to_x, "red", along_x)
    to_mid = hop(sums, 0, [r0b], 1, after=(keep1,))
    mid_b = lax.ppermute(to_mid, "blk", middle)
    at = ints(1, stays, end, end, end, end)
    keep2, to_x = ladder_call(rest, ladder_ints, at, True, after=(to_mid,), columns=2)
    x2 = lax.ppermute(to_x, "red", along_x)
    to_outer, s2 = hop(sums, 2, [mid_a, mid_b], parts=2, through=(s2,), after=(keep2,), weight=0, trailer=WIDE)
    r2 = lax.ppermute(s2, "blk", inward)
    outer = lax.ppermute(to_outer, "blk", outward)
    near = jnp.where(red // 2 == chip // 2, 1, 0)
    to_y1 = turn(ints(1 - near), (keep0, x0), (keep1, x1), 0, after=(to_outer,), weight=0, trailer=6 * TRAILER)
    y1 = lax.ppermute(to_y1, "red", along_y)
    to_inner = hop(sums, 1, [r1], parts=2, after=(to_y1,), weight=8)
    inner = lax.ppermute(to_inner, "blk", middle)
    to_y2 = turn(ints(1 - near), (keep0, x0), (keep2, x2), 1, after=(to_inner,), weight=0)
    y2 = lax.ppermute(to_y2, "red", along_y)

    orbital_ids = jnp.arange(occ_energy.shape[0], dtype=jnp.int32)
    chosen = slab_index[:, None] == orbital_ids[None, :]
    slab_energy = jnp.sum(jnp.where(chosen, occ_energy[None, :], jnp.float32(0.0)), axis=1)
    pair_energy = lax.dynamic_slice_in_dim(occ_energy, red * occ_red, occ_red)
    first_virtual = lax.dynamic_slice_in_dim(vir_energy, blk * vir_block, vir_block)
    base = first_virtual[:, None] + vir_energy[None, :]
    at = ints(near, core)
    shape = (slab, occ_red, vir_block, virt)
    settled = settle(at, shape, sums, outer, (keep0, x0), [(keep1, x1), (keep2, x2)], [y1, y2])
    return finish(at, slab_energy, pair_energy, base, settled, [r2, inner])


def plain_shards(amplitudes, ladder_ints, cycle_ints, occ_energy, vir_energy, slab_index):
    slab_rows, occ_local, vir_local, virt_width = amplitudes.shape
    occ_all = occ_local * lax.axis_size("blk")
    occ_red = occ_all // lax.axis_size("red")
    shard_piece = lax.all_gather(amplitudes, "blk", axis=1, tiled=True)
    row_count = shard_piece.shape[1]
    flattened = shard_piece.reshape(slab_rows * row_count, vir_local * virt_width)
    product = jnp.dot(flattened, ladder_ints, preferred_element_type=jnp.float32)
    ladder = product.reshape(slab_rows, row_count, ladder_ints.shape[1])
    ladder_own = lax.psum_scatter(ladder, "red", scatter_dimension=1, tiled=True)
    ladder_own = ladder_own.reshape(slab_rows, occ_red, -1, virt_width)
    shard_piece = lax.all_gather(amplitudes, "red", axis=2, tiled=True)
    vir_count = shard_piece.shape[2]
    operand = jnp.transpose(shard_piece, (0, 2, 1, 3)).reshape(slab_rows * vir_count, occ_local * virt_width)
    product = jnp.dot(operand, cycle_ints, preferred_element_type=jnp.float32)
    cycle_term = product.reshape(slab_rows, vir_count, cycle_ints.shape[1])
    cycle_own = lax.psum_scatter(cycle_term, "blk", scatter_dimension=1, tiled=True)
    vir_block = cycle_own.shape[1]
    cycle_own = jnp.transpose(cycle_own.reshape(slab_rows, vir_block, occ_red, virt_width), (0, 2, 1, 3))
    return (ladder_own + cycle_own) / denominators(occ_energy, vir_energy, slab_index, occ_red, vir_block)


def solution(mesh):
    placed = (P(None, "blk", "red", None), P("red", "blk"), P("blk", "red"), P(), P(), P())
    shards = paired_shards if (mesh.shape["blk"], mesh.shape["red"]) == (8, 4) else plain_shards
    return jax.shard_map(
        shards, mesh=mesh, in_specs=placed, out_specs=P(None, "red", "blk", None), check_vma=False
    )
```

```python
import functools

import jax
import jax.numpy as jnp
from jax import lax
from jax.experimental import pallas as pl
from jax.experimental.pallas import tpu as pltpu
from jax.sharding import PartitionSpec as P

TRAILER = 16
WIDE = 32
STEPS = 64.0
TOP = 32000.0
VMEM = 63 * 2**20 + 2**19


def encode(groups, last):
    rows = lax.broadcasted_iota(jnp.int32, (last, groups[0].shape[1]), 0)
    trailer = jnp.zeros_like(rows)
    parts = []
    for index, group in enumerate(groups):
        largest = jnp.maximum(jnp.max(jnp.abs(group), axis=0, keepdims=True), 1e-35)
        level = jnp.ceil(jnp.log(largest) * (STEPS / 0.6931471805599453))
        scaled = group * (TOP * jnp.exp2(level * (-1.0 / STEPS)))
        parts.append(jnp.round(scaled).astype(jnp.int32).astype(jnp.int16))
        trailer = jnp.where(rows == index, level.astype(jnp.int32), trailer)
    return parts, trailer.astype(jnp.int16)


def put(ref, groups, last=TRAILER):
    parts, trailer = encode(groups, last)
    row = 0
    for part in parts:
        ref[row : row + part.shape[0], :] = part
        row += part.shape[0]
    ref[row : row + last, :] = trailer


def take(ref, groups, index, last=TRAILER):
    rows = (ref.shape[0] - last) // groups
    trailer = ref[groups * rows :, :].astype(jnp.int32).astype(jnp.float32)
    scale = jnp.exp2(trailer[index : index + 1, :] * (1.0 / STEPS)) * (1.0 / TOP)
    return ref[index * rows : (index + 1) * rows, :].astype(jnp.int32).astype(jnp.float32) * scale


def params():
    return pltpu.CompilerParams(vmem_limit_bytes=VMEM, dimension_semantics=("arbitrary",))


def light(weight=0):
    return pl.CostEstimate(flops=weight * 1150000000 + 1000, bytes_accessed=1000, transcendentals=0)


def bring(candidates, code, target, sem):
    def start(source):
        return lambda: pltpu.make_async_copy(source, target, sem).start()

    if len(candidates) == 1:
        start(candidates[0])()
    else:
        for number, source in enumerate(candidates):
            pl.when(code == number)(start(source))
    return pltpu.make_async_copy(candidates[0], target, sem)


ANY = pl.BlockSpec(memory_space=pl.ANY)


def forward_kernel(rx_ref, ry_ref, *refs, skip):
    on_y_ref, on_x_ref, sems = refs[skip], refs[skip + 1], refs[-1]
    rows = on_y_ref.shape[0]
    copies = [
        pltpu.make_async_copy(rx_ref.at[pl.ds(0, rows), :], on_y_ref, sems.at[0]),
        pltpu.make_async_copy(ry_ref.at[pl.ds(rows, rows), :], on_x_ref, sems.at[1]),
    ]
    for copy in copies:
        copy.start()
    for copy in copies:
        copy.wait()


def forward(rx, ry, through=(), after=()):
    rows, width = rx.shape[0] // 2, rx.shape[1]
    block = jax.ShapeDtypeStruct((rows, width), rx.dtype)
    return pl.pallas_call(
        functools.partial(forward_kernel, skip=len(through) + len(after)),
        grid=(1,),
        in_specs=[ANY] * (2 + len(through) + len(after)),
        out_specs=[pl.BlockSpec((rows, width), lambda n: (0, 0))] * 2 + [ANY] * len(through),
        scratch_shapes=[pltpu.SemaphoreType.DMA((2,))],
        out_shape=[block, block] + [jax.ShapeDtypeStruct(t.shape, t.dtype) for t in through],
        input_output_aliases={2 + k: 2 + k for k in range(len(through))},
        compiler_params=params(),
        cost_estimate=light(),
    )(rx, ry, *through, *after)


BLOCKS = 4
SENT = 3
PARTS = 2


def cycle_kernel(at_ref, own_ref, rx_ref, ry_ref, ry2_ref, rx2_ref, left_ref, right_ref, *refs, keeps, skip):
    if keeps:
        got_ref = refs[0]
        sums_ref, s0_ref, s1_ref, s2_ref, x_ref, sems = refs[1 + skip :]
    else:
        out_ref, x_ref, sems = refs[skip:]
    rows = ry2_ref.shape[0]
    half = at_ref[0]

    @pl.when(pl.program_id(0) == 0)
    def _():
        waits = []
        place = pl.ds(pl.multiple_of(half * rows, rows), rows)
        for n in range(BLOCKS):
            target, sem = x_ref.at[pl.ds(n * rows, rows), :], sems.at[n]
            sources = [own_ref.at[place, :], rx_ref.at[place, :], ry_ref.at[place, :], ry2_ref, rx2_ref]
            code = at_ref[1 + n]
            waits.append(bring(sources, jnp.where(code == 3, 3 + half, code), target, sem))
        for copy in waits:
            copy.wait()

    products = [jnp.dot(x_ref[...], w[...], preferred_element_type=jnp.float32) for w in (left_ref, right_ref)]
    groups = [[p[rows * n : rows * (n + 1)] for p in products] for n in range(BLOCKS)]
    if not keeps:
        put(out_ref, [g for pair in groups for g in pair])
        return
    for n, pair in enumerate(groups):
        totals = [g + take(got_ref, 2 * BLOCKS, 2 * n + side) for side, g in enumerate(pair)]
        for side, total in enumerate(totals):
            sums_ref[n, rows * side : rows * (side + 1), :] = total
        if n < SENT:
            put((s0_ref, s1_ref, s2_ref)[n], totals, WIDE if n == SENT - 1 else TRAILER)


def cycle_call(sources, w, at, part, got=None, before=(), after=(), tile=256):
    own, depth = sources[0].shape
    rows, width = own // 2, w.shape[1] // 2
    tiles = width // tile // PARTS
    first = part * tiles
    operands = [*sources, w, w]
    specs = [ANY] * len(sources) + [
        pl.BlockSpec((depth, tile), lambda n, at: (0, first + n)),
        pl.BlockSpec((depth, tile), lambda n, at: (0, PARTS * tiles + first + n)),
    ]
    given = pl.BlockSpec((2 * BLOCKS * rows + TRAILER, tile), lambda n, at: (0, n))
    aliases = {}
    if got is None:
        out_shape = jax.ShapeDtypeStruct((2 * BLOCKS * rows + TRAILER, width // PARTS), jnp.int16)
        out_specs = given
    else:
        operands.append(got)
        specs.append(given)
        if before:
            aliases = {1 + len(operands): 0, 2 + len(operands): 2, 3 + len(operands): 3}
        out_shape = [
            jax.ShapeDtypeStruct((BLOCKS, own, width), jnp.float32),
            jax.ShapeDtypeStruct((own + TRAILER, width // PARTS), jnp.int16),
            jax.ShapeDtypeStruct((own + TRAILER, width), jnp.int16),
            jax.ShapeDtypeStruct((own + WIDE, width), jnp.int16),
        ]
        out_specs = [
            pl.BlockSpec((BLOCKS, own, tile), lambda n, at: (0, 0, first + n)),
            pl.BlockSpec((own + TRAILER, tile), lambda n, at: (0, n)),
            pl.BlockSpec((own + TRAILER, tile), lambda n, at: (0, first + n)),
            pl.BlockSpec((own + WIDE, tile), lambda n, at: (0, first + n)),
        ]
    skip = len(before) + len(after)
    return pl.pallas_call(
        functools.partial(cycle_kernel, keeps=got is not None, skip=skip),
        grid_spec=pltpu.PrefetchScalarGridSpec(
            num_scalar_prefetch=1,
            grid=(tiles,),
            in_specs=specs + [ANY] * skip,
            out_specs=out_specs,
            scratch_shapes=[pltpu.VMEM((BLOCKS * rows, depth), jnp.bfloat16), pltpu.SemaphoreType.DMA((BLOCKS,))],
        ),
        out_shape=out_shape,
        input_output_aliases=aliases,
        compiler_params=params(),
        cost_estimate=light(19),
    )(at, *operands, *before, *after)


def gate_kernel(*refs):
    refs[-1][...] = jnp.zeros_like(refs[-1])


def gate(*through, after=()):
    out = pl.pallas_call(
        gate_kernel,
        in_specs=[ANY] * (len(through) + len(after)),
        out_specs=[ANY] * len(through) + [pl.BlockSpec(memory_space=pltpu.VMEM)],
        out_shape=[jax.ShapeDtypeStruct(t.shape, t.dtype) for t in through] + [jax.ShapeDtypeStruct((8, 128), jnp.float32)],
        input_output_aliases={k: k for k in range(len(through))},
        cost_estimate=light(),
    )(*through, *after)
    return out[:-1]


def hop_kernel(base_ref, *refs, joins, skip, trailer):
    rows = base_ref.shape[1] // 2

    def send(got_ref):
        put(refs[joins + skip], [base_ref[0, rows * g : rows * (g + 1), :] + take(got_ref, 2, g) for g in range(2)], trailer)

    if joins == 1:
        send(refs[0])
    else:
        for part in range(joins):
            pl.when(pl.program_id(0) == part)(functools.partial(send, refs[part]))


def hop(sums, place, got, part=0, parts=1, through=(), after=(), weight=4, trailer=TRAILER):
    rows, tile = sums.shape[1], sums.shape[2] // 2
    joins = len(got)
    skip = len(through) + len(after)
    index = (lambda n: (0, n)) if joins == 1 else (lambda n: (0, 0))
    out = pl.pallas_call(
        functools.partial(hop_kernel, joins=joins, skip=skip, trailer=trailer),
        grid=(parts,),
        in_specs=[pl.BlockSpec((1, rows, tile), lambda n: (place, 0, part + n))]
        + [pl.BlockSpec((rows + TRAILER, tile), index)] * joins
        + [ANY] * skip,
        out_specs=[pl.BlockSpec((rows + trailer, tile), lambda n: (0, n))] + [ANY] * len(through),
        out_shape=[jax.ShapeDtypeStruct((rows + trailer, parts * tile), jnp.int16)]
        + [jax.ShapeDtypeStruct(t.shape, t.dtype) for t in through],
        input_output_aliases={1 + joins + k: 1 + k for k in range(len(through))},
        compiler_params=params(),
        cost_estimate=light(weight),
    )(sums, *got, *through, *after)
    return out if through else out[0]


def fill(at_ref, first_code, groups, refs, x_ref, sems):
    @pl.when(pl.program_id(0) == 0)
    def _():
        waits, row, used = [], 0, 0
        for index, count in enumerate(groups):
            rows = refs[used].shape[0]
            target = x_ref.at[pl.ds(row, rows), :]
            waits.append(bring(refs[used : used + count], at_ref[first_code + index], target, sems.at[index]))
            row, used = row + rows, used + count
        for copy in waits:
            copy.wait()


def ladder_one_kernel(at_ref, *refs, groups, after):
    sources, w_ref = refs[: sum(groups)], refs[sum(groups)]
    out_ref, x_ref, sems = refs[sum(groups) + 1 + after :]
    fill(at_ref, 2, groups, sources, x_ref, sems)
    out_ref[...] = jnp.dot(x_ref[...], w_ref[...], preferred_element_type=jnp.float32)


def ladder_pair_kernel(at_ref, *refs, groups, after, prior, trailer):
    sources, w_ref = refs[: sum(groups)], refs[sum(groups)]
    prior_ref = refs[sum(groups) + 1]
    keep_ref, message_ref, x_ref, sems, part_ref = refs[sum(groups) + 1 + prior + after :]
    fill(at_ref, 2, groups, sources, x_ref, sems)
    product = jnp.dot(x_ref[...], w_ref[...], preferred_element_type=jnp.float32)
    rows = keep_ref.shape[1]
    if prior:
        part_ref[0] = prior_ref[...]
        part_ref[1] = product
    else:
        part_ref[0] = product[:rows]
        part_ref[1] = product[rows:]
    keep_ref[0] = part_ref[at_ref[1]]
    put(message_ref, [part_ref[1 - at_ref[1]]], trailer)


def ladder_call(groups, w, at, pair, prior=None, after=(), columns=1, trailer=TRAILER, tile=512):
    depth = groups[0][0].shape[1]
    total = sum(g[0].shape[0] for g in groups)
    width = w.shape[1] // columns
    tiles = width // tile
    counts = tuple(len(g) for g in groups)
    operands = [a for g in groups for a in g] + [w]
    specs = [ANY] * sum(counts) + [pl.BlockSpec((depth, tile), lambda n, at: (0, at[0] * tiles + n))]
    scratch = [pltpu.VMEM((total, depth), jnp.bfloat16), pltpu.SemaphoreType.DMA((len(counts),))]
    if pair:
        rows = total if prior is not None else total // 2
        if prior is not None:
            operands.append(prior)
            specs.append(pl.BlockSpec((rows, tile), lambda n, at: (0, at[0] * tiles + n)))
        kernel = functools.partial(ladder_pair_kernel, groups=counts, after=len(after), prior=int(prior is not None), trailer=trailer)
        out_shape = [
            jax.ShapeDtypeStruct((1, rows, width), jnp.float32),
            jax.ShapeDtypeStruct((rows + trailer, width), jnp.int16),
        ]
        out_specs = [
            pl.BlockSpec((1, rows, tile), lambda n, at: (0, 0, n)),
            pl.BlockSpec((rows + trailer, tile), lambda n, at: (0, n)),
        ]
        scratch.append(pltpu.VMEM((2, rows, tile), jnp.float32))
    else:
        kernel = functools.partial(ladder_one_kernel, groups=counts, after=len(after))
        out_shape = jax.ShapeDtypeStruct((total, width), jnp.float32)
        out_specs = pl.BlockSpec((total, tile), lambda n, at: (0, n))
    return pl.pallas_call(
        kernel,
        grid_spec=pltpu.PrefetchScalarGridSpec(
            num_scalar_prefetch=1,
            grid=(tiles,),
            in_specs=specs + [ANY] * len(after),
            out_specs=out_specs,
            scratch_shapes=scratch,
        ),
        out_shape=out_shape,
        compiler_params=params(),
        cost_estimate=light(),
    )(at, *operands, *after)


def turn_kernel(at_ref, *refs, trailer):
    for near, (base_ref, got_ref) in enumerate((refs[2:4], refs[0:2])):

        @pl.when(at_ref[0] == near)
        def _(near=near, base_ref=base_ref, got_ref=got_ref):
            put(refs[-1], [base_ref[0] + take(got_ref, 1, 0, WIDE if near else TRAILER)], trailer)


def turn(at, chunk0, chunk1, part, after=(), weight=4, trailer=TRAILER):
    _, rows, width = chunk1[0].shape
    operands, specs = [], []
    for (keep, got), index in ((chunk0, part), (chunk1, 0)):
        operands += [keep, got]
        specs.append(pl.BlockSpec((1, rows, width), lambda n, at, index=index: (0, 0, index)))
        specs.append(pl.BlockSpec((got.shape[0], width), lambda n, at, index=index: (0, index)))
    return pl.pallas_call(
        functools.partial(turn_kernel, trailer=trailer),
        grid_spec=pltpu.PrefetchScalarGridSpec(
            num_scalar_prefetch=1,
            grid=(1,),
            in_specs=specs + [ANY] * len(after),
            out_specs=pl.BlockSpec((rows + trailer, width), lambda n, at: (0, n)),
        ),
        out_shape=jax.ShapeDtypeStruct((rows + trailer, width), jnp.int16),
        compiler_params=params(),
        cost_estimate=light(weight),
    )(at, *operands, *after)


def scaled(message, side, group):
    trailer = message[2][group : group + 1, :].astype(jnp.int32).astype(jnp.float32)
    scale = jnp.exp2(trailer * (1.0 / STEPS)) * (1.0 / TOP)
    return message[side][...].astype(jnp.int32).astype(jnp.float32) * scale


class Blocks:
    def __init__(self, steps):
        self.steps, self.operands, self.specs = steps, [], []

    def add(self, array, shape, index):
        self.operands.append(array)
        self.specs.append(pl.BlockSpec(shape, index))

    def place(self, at, side, n, near):
        place = side * self.steps + n
        return place if near is None else jnp.where(at[0] == near, place, 0)

    def message(self, array, trailer, near=None):
        rows, width = (array.shape[0] - trailer) // 2 // self.steps, array.shape[1]
        for side in range(2):
            self.add(array, (rows, width), lambda n, at, *_, side=side: (self.place(at, side, n, near), 0))
        last = (array.shape[0] - trailer) // trailer
        self.add(array, (trailer, width), lambda n, *_: (last, 0))

    def sides(self, array, first, near=None):
        rows, width = array.shape[1] // 2 // self.steps, array.shape[2]
        for side in range(2):
            self.add(array, (1, rows, width), lambda n, at, *_, side=side: (first, self.place(at, side, n, near), 0))


def settle_kernel(at_ref, *refs):
    *refs, out_ref, cycle_ref, ladder_ref = refs
    near, core = at_ref[0], at_ref[1]
    refs = list(refs)

    def next_refs(count):
        return [refs.pop(0) for _ in range(count)]

    base, chain = next_refs(2), next_refs(3)
    for side in range(2):
        cycle_ref[side] = base[side][0] + scaled(chain, side, side)

    slab, occ, block, lanes = out_ref.shape
    keep0, x0 = next_refs(2), next_refs(3)
    chunk1 = [(next_refs(2), next_refs(3)) for _ in range(2)]
    came = [next_refs(3) for _ in range(2)]
    rows = keep0[0].shape[1]

    def spread(part, side, total):
        total = total + scaled(came[part], side, 0)
        for a in range(block // 2):
            row = ((part * (block // 2) + a) * 2 + side) * rows
            ladder_ref[row : row + rows, :] = total[:, a * lanes : (a + 1) * lanes]

    @pl.when(near == 1)
    def _():
        for side in range(2):
            total = keep0[side][0] + scaled(x0, side, 0)
            half = total.shape[1] // 2
            for part in range(2):
                spread(part, side, total[:, part * half : (part + 1) * half])

    @pl.when(near != 1)
    def _():
        for part, (keep, got) in enumerate(chunk1):
            for side in range(2):
                spread(part, side, keep[side][0] + scaled(got, side, 0))

    per = occ // 2

    def row(i, carry):
        for side in range(2):
            first = jnp.where(core == side, 0, rows)
            for j in range(per):
                ladder = ladder_ref[pl.ds(first + i * per + j, block, stride=2 * rows), :]
                place = pl.ds(pl.multiple_of(i * block, block), block)
                out_ref[i, side * per + j] = ladder + cycle_ref[side, place, j * lanes : (j + 1) * lanes]
        return carry

    lax.fori_loop(0, slab, row, 0)


def settle(at, shape, sums, outer, chunk0, chunk1, came, steps=4):
    slab, occ, vir, lanes = shape
    mine, wide = sums.shape[1] // 2 // steps, sums.shape[2]
    blocks = Blocks(steps)
    blocks.sides(sums, SENT)
    blocks.message(outer, WIDE)
    blocks.sides(chunk0[0], 0, 1)
    blocks.message(chunk0[1], WIDE, 1)
    for keep, got in chunk1:
        blocks.sides(keep, 0, 0)
        blocks.message(got, TRAILER, 0)
    for array in came:
        blocks.message(array, array.shape[0] - chunk0[0].shape[1])
    rows = chunk0[0].shape[1] // 2 // steps
    return pl.pallas_call(
        settle_kernel,
        grid_spec=pltpu.PrefetchScalarGridSpec(
            num_scalar_prefetch=1,
            grid=(steps,),
            in_specs=blocks.specs,
            out_specs=pl.BlockSpec((slab // steps, occ, vir, lanes), lambda n, *_: (n, 0, 0, 0)),
            scratch_shapes=[
                pltpu.VMEM((2, mine, wide), jnp.float32),
                pltpu.VMEM((2 * vir * rows, lanes), jnp.float32),
            ],
        ),
        out_shape=jax.ShapeDtypeStruct(shape, jnp.float32),
        compiler_params=params(),
        cost_estimate=light(7),
    )(at, *blocks.operands)


def finish_kernel(at_ref, slab_ref, pair_ref, base_ref, settled_ref, *refs):
    first, second = refs[0:3], refs[3:6]
    out_ref, cycle_ref = refs[6:]
    for side in range(2):
        cycle_ref[side] = scaled(first, side, side) + scaled(second, side, side)
    slab, occ, block, lanes = out_ref.shape
    per = occ // 2
    step = pl.program_id(0)

    def row(i, carry):
        energy = base_ref[...] - slab_ref[step * slab + i]
        place = pl.ds(pl.multiple_of(i * block, block), block)
        for side in range(2):
            for j in range(per):
                total = settled_ref[i, side * per + j] + cycle_ref[side, place, j * lanes : (j + 1) * lanes]
                out_ref[i, side * per + j] = total / (energy - pair_ref[side * per + j])
        return carry

    lax.fori_loop(0, slab, row, 0)


def finish(at, slab_energy, pair_energy, base, settled, cycle, steps=2):
    slab, occ, vir, lanes = settled.shape
    blocks = Blocks(steps)
    blocks.add(base, base.shape, lambda n, *_: (0, 0))
    blocks.add(settled, (slab // steps, occ, vir, lanes), lambda n, *_: (n, 0, 0, 0))
    for array, trailer in zip(cycle, (WIDE, TRAILER)):
        blocks.message(array, trailer)
    wide = cycle[0].shape[1]
    return pl.pallas_call(
        finish_kernel,
        grid_spec=pltpu.PrefetchScalarGridSpec(
            num_scalar_prefetch=3,
            grid=(steps,),
            in_specs=blocks.specs,
            out_specs=pl.BlockSpec((slab // steps, occ, vir, lanes), lambda n, *_: (n, 0, 0, 0)),
            scratch_shapes=[pltpu.VMEM((2, slab * vir // steps, wide), jnp.float32)],
        ),
        out_shape=jax.ShapeDtypeStruct(settled.shape, jnp.float32),
        compiler_params=params(),
        cost_estimate=light(),
    )(at, slab_energy, pair_energy, *blocks.operands)


def denominators(occ_energy, vir_energy, slab_index, occ_red, vir_block):
    orbital_ids = jnp.arange(occ_energy.shape[0], dtype=jnp.int32)
    chosen = slab_index[:, None] == orbital_ids[None, :]
    slab_energy = jnp.sum(jnp.where(chosen, occ_energy[None, :], jnp.float32(0.0)), axis=1)
    pair_energy = lax.dynamic_slice_in_dim(occ_energy, lax.axis_index("red") * occ_red, occ_red)
    first_virtual = lax.dynamic_slice_in_dim(vir_energy, lax.axis_index("blk") * vir_block, vir_block)
    return (
        first_virtual[None, None, :, None]
        + vir_energy[None, None, None, :]
        - slab_energy[:, None, None, None]
        - pair_energy[None, :, None, None]
    )


ORDER = ((3, 2, 1, 0), (3, 2, 0, 1), (0, 1, 3, 2), (0, 1, 2, 3))


def paired_shards(amplitudes, ladder_ints, cycle_ints, occ_energy, vir_energy, slab_index):
    slab, occ_local, vir_local, virt = amplitudes.shape
    blk, red = lax.axis_index("blk"), lax.axis_index("red")
    chip, core = blk // 2, blk % 2
    x_place = red % 2
    along_x = [(r, r ^ 1) for r in range(4)]
    along_y = [(r, r ^ 2) for r in range(4)]
    across = [(b, b ^ 1) for b in range(8)]

    def line(*hops):
        return [(2 * a + c, 2 * b + c) for a, b in hops for c in range(2)]

    inward, middle, outward = line((0, 1), (3, 2)), line((1, 2), (2, 1)), line((1, 0), (2, 3))

    def ints(*values):
        return jnp.stack([jnp.asarray(v, jnp.int32) for v in values])

    occ_red, vir_block = 2 * occ_local, vir_local // 2
    zeros = jnp.zeros((8,), jnp.int32)

    mine = amplitudes.reshape(slab, occ_local, 2, vir_block, virt)
    mine = jnp.transpose(mine, (2, 0, 3, 1, 4)).reshape(2 * slab * vir_block, occ_local * virt)
    rx = lax.ppermute(mine, "red", along_x)
    ry = lax.ppermute(mine, "red", along_y)

    own = amplitudes.reshape(slab * occ_local, vir_local * virt)
    g1 = lax.ppermute(own, "blk", line((0, 1), (1, 0), (2, 3), (3, 2)))
    g2 = lax.ppermute(own, "blk", middle)
    own_s = lax.ppermute(own, "blk", across)
    p_own = ladder_call([[own], [own_s]], ladder_ints, zeros, False)

    on_y, on_x, g1, g2 = forward(rx, ry, through=(g1, g2), after=(p_own,))
    rx2 = lax.ppermute(on_x, "red", along_x)
    ry2 = lax.ppermute(on_y, "red", along_y)
    g3 = lax.ppermute(g1, "blk", middle)
    g4 = lax.ppermute(g2, "blk", outward)
    g1_s = lax.ppermute(g1, "blk", across)
    g2_s = lax.ppermute(g2, "blk", across)
    g3_s = lax.ppermute(g3, "blk", across)
    g4_s = lax.ppermute(g4, "blk", across)
    near_x = ints(0, jnp.where(x_place == chip % 2, 0, 1), 0, 0)
    keep0, to_x = ladder_call([[g1], [g1_s]], ladder_ints, near_x, True, prior=p_own, trailer=WIDE)
    x0 = lax.ppermute(to_x, "red", along_x)

    blocks = [mine, rx, ry, ry2, rx2]
    places = jnp.array(ORDER, jnp.int32)[chip] ^ red
    at_give, at_keep = jnp.concatenate([ints(1 - core), places]), jnp.concatenate([ints(core), places])
    give_a = cycle_call(blocks, cycle_ints, at_give, 0, after=(keep0, g2_s))
    got_a = lax.ppermute(give_a, "blk", across)
    give_b = cycle_call(blocks, cycle_ints, at_give, 1, after=(give_a, g3, g4))
    got_b = lax.ppermute(give_b, "blk", across)
    sums, s0a, s1, s2 = cycle_call(blocks, cycle_ints, at_keep, 0, got_a, after=(give_b,))
    r0a = lax.ppermute(s0a, "blk", inward)
    sums, s0b, s1, s2 = cycle_call(blocks, cycle_ints, at_keep, 1, got_b, (sums, s1, s2))
    r0b = lax.ppermute(s0b, "blk", inward)
    g5 = lax.ppermute(g3, "blk", outward)

    s1, s2, g5 = gate(s1, s2, g5, after=(sums, r0a))
    to_mid = hop(sums, 0, [r0a], 0, after=(s1,))
    g5_s = lax.ppermute(g5, "blk", across)
    mid_a = lax.ppermute(to_mid, "blk", middle)
    r1 = lax.ppermute(s1, "blk", inward)
    end = jnp.where((chip == 0) | (chip == 3), 1, 0)
    stays = jnp.where(x_place == chip // 2, 0, 1)
    rest = [[g2, g4], [g2_s, g4_s], [g3, g5], [g3_s, g5_s]]
    at = ints(0, stays, end, end, end, end)
    keep1, to_x = ladder_call(rest, ladder_ints, at, True, after=(to_mid, x0), columns=2)
    x1 = lax.ppermute(to_x, "red", along_x)
    to_mid = hop(sums, 0, [r0b], 1, after=(keep1,))
    mid_b = lax.ppermute(to_mid, "blk", middle)
    at = ints(1, stays, end, end, end, end)
    keep2, to_x = ladder_call(rest, ladder_ints, at, True, after=(to_mid,), columns=2)
    x2 = lax.ppermute(to_x, "red", along_x)
    to_outer, s2 = hop(sums, 2, [mid_a, mid_b], parts=2, through=(s2,), after=(keep2,), weight=0, trailer=WIDE)
    r2 = lax.ppermute(s2, "blk", inward)
    outer = lax.ppermute(to_outer, "blk", outward)
    near = jnp.where(red // 2 == chip // 2, 1, 0)
    to_y1 = turn(ints(1 - near), (keep0, x0), (keep1, x1), 0, after=(to_outer,), weight=0, trailer=6 * TRAILER)
    y1 = lax.ppermute(to_y1, "red", along_y)
    to_inner = hop(sums, 1, [r1], parts=2, after=(to_y1,), weight=8)
    inner = lax.ppermute(to_inner, "blk", middle)
    to_y2 = turn(ints(1 - near), (keep0, x0), (keep2, x2), 1, after=(to_inner,), weight=0)
    y2 = lax.ppermute(to_y2, "red", along_y)

    orbital_ids = jnp.arange(occ_energy.shape[0], dtype=jnp.int32)
    chosen = slab_index[:, None] == orbital_ids[None, :]
    slab_energy = jnp.sum(jnp.where(chosen, occ_energy[None, :], jnp.float32(0.0)), axis=1)
    pair_energy = lax.dynamic_slice_in_dim(occ_energy, red * occ_red, occ_red)
    first_virtual = lax.dynamic_slice_in_dim(vir_energy, blk * vir_block, vir_block)
    base = first_virtual[:, None] + vir_energy[None, :]
    at = ints(near, core)
    shape = (slab, occ_red, vir_block, virt)
    settled = settle(at, shape, sums, outer, (keep0, x0), [(keep1, x1), (keep2, x2)], [y1, y2])
    return finish(at, slab_energy, pair_energy, base, settled, [r2, inner])


def plain_shards(amplitudes, ladder_ints, cycle_ints, occ_energy, vir_energy, slab_index):
    slab_rows, occ_local, vir_local, virt_width = amplitudes.shape
    occ_all = occ_local * lax.axis_size("blk")
    occ_red = occ_all // lax.axis_size("red")
    shard_piece = lax.all_gather(amplitudes, "blk", axis=1, tiled=True)
    row_count = shard_piece.shape[1]
    flattened = shard_piece.reshape(slab_rows * row_count, vir_local * virt_width)
    product = jnp.dot(flattened, ladder_ints, preferred_element_type=jnp.float32)
    ladder = product.reshape(slab_rows, row_count, ladder_ints.shape[1])
    ladder_own = lax.psum_scatter(ladder, "red", scatter_dimension=1, tiled=True)
    ladder_own = ladder_own.reshape(slab_rows, occ_red, -1, virt_width)
    shard_piece = lax.all_gather(amplitudes, "red", axis=2, tiled=True)
    vir_count = shard_piece.shape[2]
    operand = jnp.transpose(shard_piece, (0, 2, 1, 3)).reshape(slab_rows * vir_count, occ_local * virt_width)
    product = jnp.dot(operand, cycle_ints, preferred_element_type=jnp.float32)
    cycle_term = product.reshape(slab_rows, vir_count, cycle_ints.shape[1])
    cycle_own = lax.psum_scatter(cycle_term, "blk", scatter_dimension=1, tiled=True)
    vir_block = cycle_own.shape[1]
    cycle_own = jnp.transpose(cycle_own.reshape(slab_rows, vir_block, occ_red, virt_width), (0, 2, 1, 3))
    return (ladder_own + cycle_own) / denominators(occ_energy, vir_energy, slab_index, occ_red, vir_block)


def solution(mesh):
    placed = (P(None, "blk", "red", None), P("red", "blk"), P("blk", "red"), P(), P(), P())
    shards = paired_shards if (mesh.shape["blk"], mesh.shape["red"]) == (8, 4) else plain_shards
    return jax.shard_map(
        shards, mesh=mesh, in_specs=placed, out_specs=P(None, "red", "blk", None), check_vma=False
    )
```

```python
import functools

import jax
import jax.numpy as jnp
from jax import lax
from jax.experimental import pallas as pl
from jax.experimental.pallas import tpu as pltpu
from jax.sharding import PartitionSpec as P

TRAILER = 16
WIDE = 32
STEPS = 64.0
TOP = 32000.0
VMEM = 63 * 2**20 + 2**19


def encode(groups, last):
    rows = lax.broadcasted_iota(jnp.int32, (last, groups[0].shape[1]), 0)
    trailer = jnp.zeros_like(rows)
    parts = []
    for index, group in enumerate(groups):
        largest = jnp.maximum(jnp.max(jnp.abs(group), axis=0, keepdims=True), 1e-35)
        level = jnp.ceil(jnp.log(largest) * (STEPS / 0.6931471805599453))
        scaled = group * (TOP * jnp.exp2(level * (-1.0 / STEPS)))
        parts.append(jnp.round(scaled).astype(jnp.int32).astype(jnp.int16))
        trailer = jnp.where(rows == index, level.astype(jnp.int32), trailer)
    return parts, trailer.astype(jnp.int16)


def put(ref, groups, last=TRAILER):
    parts, trailer = encode(groups, last)
    row = 0
    for part in parts:
        ref[row : row + part.shape[0], :] = part
        row += part.shape[0]
    ref[row : row + last, :] = trailer


def take(ref, groups, index, last=TRAILER):
    rows = (ref.shape[0] - last) // groups
    trailer = ref[groups * rows :, :].astype(jnp.int32).astype(jnp.float32)
    scale = jnp.exp2(trailer[index : index + 1, :] * (1.0 / STEPS)) * (1.0 / TOP)
    return ref[index * rows : (index + 1) * rows, :].astype(jnp.int32).astype(jnp.float32) * scale


def params():
    return pltpu.CompilerParams(vmem_limit_bytes=VMEM, dimension_semantics=("arbitrary",))


def light(weight=0):
    return pl.CostEstimate(flops=int(weight * 1.15e9) + 1000, bytes_accessed=1000, transcendentals=0)


def bring(candidates, code, target, sem):
    def start(source):
        return lambda: pltpu.make_async_copy(source, target, sem).start()

    if len(candidates) == 1:
        start(candidates[0])()
    else:
        for number, source in enumerate(candidates):
            pl.when(code == number)(start(source))
    return pltpu.make_async_copy(candidates[0], target, sem)


ANY = pl.BlockSpec(memory_space=pl.ANY)


def forward_kernel(rx_ref, ry_ref, *refs, skip):
    on_y_ref, on_x_ref, sems = refs[skip], refs[skip + 1], refs[-1]
    rows = on_y_ref.shape[0]
    copies = [
        pltpu.make_async_copy(rx_ref.at[pl.ds(0, rows), :], on_y_ref, sems.at[0]),
        pltpu.make_async_copy(ry_ref.at[pl.ds(rows, rows), :], on_x_ref, sems.at[1]),
    ]
    for copy in copies:
        copy.start()
    for copy in copies:
        copy.wait()


def forward(rx, ry, through=(), after=()):
    rows, width = rx.shape[0] // 2, rx.shape[1]
    block = jax.ShapeDtypeStruct((rows, width), rx.dtype)
    return pl.pallas_call(
        functools.partial(forward_kernel, skip=len(through) + len(after)),
        grid=(1,),
        in_specs=[ANY] * (2 + len(through) + len(after)),
        out_specs=[pl.BlockSpec((rows, width), lambda n: (0, 0))] * 2 + [ANY] * len(through),
        scratch_shapes=[pltpu.SemaphoreType.DMA((2,))],
        out_shape=[block, block] + [jax.ShapeDtypeStruct(t.shape, t.dtype) for t in through],
        input_output_aliases={2 + k: 2 + k for k in range(len(through))},
        compiler_params=params(),
        cost_estimate=light(),
    )(rx, ry, *through, *after)


BLOCKS = 4
SENT = 3
PARTS = 2


def cycle_kernel(at_ref, own_ref, rx_ref, ry_ref, ry2_ref, rx2_ref, left_ref, right_ref, *refs, keeps, skip):
    if keeps:
        got_ref = refs[0]
        sums_ref, s0_ref, s1_ref, s2_ref, x_ref, sems = refs[1 + skip :]
    else:
        out_ref, x_ref, sems = refs[skip:]
    rows = ry2_ref.shape[0]
    half = at_ref[0]

    @pl.when(pl.program_id(0) == 0)
    def _():
        waits = []
        place = pl.ds(pl.multiple_of(half * rows, rows), rows)
        for n in range(BLOCKS):
            target, sem = x_ref.at[pl.ds(n * rows, rows), :], sems.at[n]
            sources = [own_ref.at[place, :], rx_ref.at[place, :], ry_ref.at[place, :], ry2_ref, rx2_ref]
            code = at_ref[1 + n]
            waits.append(bring(sources, jnp.where(code == 3, 3 + half, code), target, sem))
        for copy in waits:
            copy.wait()

    products = [jnp.dot(x_ref[...], w[...], preferred_element_type=jnp.float32) for w in (left_ref, right_ref)]
    groups = [[p[rows * n : rows * (n + 1)] for p in products] for n in range(BLOCKS)]
    if not keeps:
        put(out_ref, [g for pair in groups for g in pair])
        return
    for n, pair in enumerate(groups):
        totals = [g + take(got_ref, 2 * BLOCKS, 2 * n + side) for side, g in enumerate(pair)]
        for side, total in enumerate(totals):
            sums_ref[n, rows * side : rows * (side + 1), :] = total
        if n < SENT:
            put((s0_ref, s1_ref, s2_ref)[n], totals, WIDE if n == SENT - 1 else TRAILER)


def cycle_call(sources, w, at, part, got=None, before=(), after=(), tile=256):
    own, depth = sources[0].shape
    rows, width = own // 2, w.shape[1] // 2
    tiles = width // tile // PARTS
    first = part * tiles
    operands = [*sources, w, w]
    specs = [ANY] * len(sources) + [
        pl.BlockSpec((depth, tile), lambda n, at: (0, first + n)),
        pl.BlockSpec((depth, tile), lambda n, at: (0, PARTS * tiles + first + n)),
    ]
    given = pl.BlockSpec((2 * BLOCKS * rows + TRAILER, tile), lambda n, at: (0, n))
    aliases = {}
    if got is None:
        out_shape = jax.ShapeDtypeStruct((2 * BLOCKS * rows + TRAILER, width // PARTS), jnp.int16)
        out_specs = given
    else:
        operands.append(got)
        specs.append(given)
        if before:
            aliases = {1 + len(operands): 0, 2 + len(operands): 2, 3 + len(operands): 3}
        out_shape = [
            jax.ShapeDtypeStruct((BLOCKS, own, width), jnp.float32),
            jax.ShapeDtypeStruct((own + TRAILER, width // PARTS), jnp.int16),
            jax.ShapeDtypeStruct((own + TRAILER, width), jnp.int16),
            jax.ShapeDtypeStruct((own + WIDE, width), jnp.int16),
        ]
        out_specs = [
            pl.BlockSpec((BLOCKS, own, tile), lambda n, at: (0, 0, first + n)),
            pl.BlockSpec((own + TRAILER, tile), lambda n, at: (0, n)),
            pl.BlockSpec((own + TRAILER, tile), lambda n, at: (0, first + n)),
            pl.BlockSpec((own + WIDE, tile), lambda n, at: (0, first + n)),
        ]
    skip = len(before) + len(after)
    return pl.pallas_call(
        functools.partial(cycle_kernel, keeps=got is not None, skip=skip),
        grid_spec=pltpu.PrefetchScalarGridSpec(
            num_scalar_prefetch=1,
            grid=(tiles,),
            in_specs=specs + [ANY] * skip,
            out_specs=out_specs,
            scratch_shapes=[pltpu.VMEM((BLOCKS * rows, depth), jnp.bfloat16), pltpu.SemaphoreType.DMA((BLOCKS,))],
        ),
        out_shape=out_shape,
        input_output_aliases=aliases,
        compiler_params=params(),
        cost_estimate=light(19),
    )(at, *operands, *before, *after)


def gate_kernel(*refs):
    refs[-1][...] = jnp.zeros_like(refs[-1])


def gate(*through, after=()):
    out = pl.pallas_call(
        gate_kernel,
        in_specs=[ANY] * (len(through) + len(after)),
        out_specs=[ANY] * len(through) + [pl.BlockSpec(memory_space=pltpu.VMEM)],
        out_shape=[jax.ShapeDtypeStruct(t.shape, t.dtype) for t in through] + [jax.ShapeDtypeStruct((8, 128), jnp.float32)],
        input_output_aliases={k: k for k in range(len(through))},
        cost_estimate=light(),
    )(*through, *after)
    return out[:-1]


def hop_kernel(base_ref, *refs, joins, skip, trailer):
    rows = base_ref.shape[1] // 2

    def send(got_ref):
        put(refs[joins + skip], [base_ref[0, rows * g : rows * (g + 1), :] + take(got_ref, 2, g) for g in range(2)], trailer)

    if joins == 1:
        send(refs[0])
    else:
        for part in range(joins):
            pl.when(pl.program_id(0) == part)(functools.partial(send, refs[part]))


def hop(sums, place, got, part=0, parts=1, through=(), after=(), weight=4, trailer=TRAILER):
    rows, tile = sums.shape[1], sums.shape[2] // 2
    joins = len(got)
    skip = len(through) + len(after)
    index = (lambda n: (0, n)) if joins == 1 else (lambda n: (0, 0))
    out = pl.pallas_call(
        functools.partial(hop_kernel, joins=joins, skip=skip, trailer=trailer),
        grid=(parts,),
        in_specs=[pl.BlockSpec((1, rows, tile), lambda n: (place, 0, part + n))]
        + [pl.BlockSpec((rows + TRAILER, tile), index)] * joins
        + [ANY] * skip,
        out_specs=[pl.BlockSpec((rows + trailer, tile), lambda n: (0, n))] + [ANY] * len(through),
        out_shape=[jax.ShapeDtypeStruct((rows + trailer, parts * tile), jnp.int16)]
        + [jax.ShapeDtypeStruct(t.shape, t.dtype) for t in through],
        input_output_aliases={1 + joins + k: 1 + k for k in range(len(through))},
        compiler_params=params(),
        cost_estimate=light(weight),
    )(sums, *got, *through, *after)
    return out if through else out[0]


def fill(at_ref, first_code, groups, refs, x_ref, sems):
    @pl.when(pl.program_id(0) == 0)
    def _():
        waits, row, used = [], 0, 0
        for index, count in enumerate(groups):
            rows = refs[used].shape[0]
            target = x_ref.at[pl.ds(row, rows), :]
            waits.append(bring(refs[used : used + count], at_ref[first_code + index], target, sems.at[index]))
            row, used = row + rows, used + count
        for copy in waits:
            copy.wait()


def ladder_one_kernel(at_ref, *refs, groups, after):
    sources, w_ref = refs[: sum(groups)], refs[sum(groups)]
    out_ref, x_ref, sems = refs[sum(groups) + 1 + after :]
    fill(at_ref, 2, groups, sources, x_ref, sems)
    out_ref[...] = jnp.dot(x_ref[...], w_ref[...], preferred_element_type=jnp.float32)


def ladder_pair_kernel(at_ref, *refs, groups, after, prior, trailer):
    sources, w_ref = refs[: sum(groups)], refs[sum(groups)]
    prior_ref = refs[sum(groups) + 1]
    keep_ref, message_ref, x_ref, sems, part_ref = refs[sum(groups) + 1 + prior + after :]
    fill(at_ref, 2, groups, sources, x_ref, sems)
    product = jnp.dot(x_ref[...], w_ref[...], preferred_element_type=jnp.float32)
    rows = keep_ref.shape[1]
    if prior:
        part_ref[0] = prior_ref[...]
        part_ref[1] = product
    else:
        part_ref[0] = product[:rows]
        part_ref[1] = product[rows:]
    keep_ref[0] = part_ref[at_ref[1]]
    put(message_ref, [part_ref[1 - at_ref[1]]], trailer)


def ladder_call(groups, w, at, pair, prior=None, after=(), columns=1, trailer=TRAILER, tile=512):
    depth = groups[0][0].shape[1]
    total = sum(g[0].shape[0] for g in groups)
    width = w.shape[1] // columns
    tiles = width // tile
    counts = tuple(len(g) for g in groups)
    operands = [a for g in groups for a in g] + [w]
    specs = [ANY] * sum(counts) + [pl.BlockSpec((depth, tile), lambda n, at: (0, at[0] * tiles + n))]
    scratch = [pltpu.VMEM((total, depth), jnp.bfloat16), pltpu.SemaphoreType.DMA((len(counts),))]
    if pair:
        rows = total if prior is not None else total // 2
        if prior is not None:
            operands.append(prior)
            specs.append(pl.BlockSpec((rows, tile), lambda n, at: (0, at[0] * tiles + n)))
        kernel = functools.partial(ladder_pair_kernel, groups=counts, after=len(after), prior=int(prior is not None), trailer=trailer)
        out_shape = [
            jax.ShapeDtypeStruct((1, rows, width), jnp.float32),
            jax.ShapeDtypeStruct((rows + trailer, width), jnp.int16),
        ]
        out_specs = [
            pl.BlockSpec((1, rows, tile), lambda n, at: (0, 0, n)),
            pl.BlockSpec((rows + trailer, tile), lambda n, at: (0, n)),
        ]
        scratch.append(pltpu.VMEM((2, rows, tile), jnp.float32))
    else:
        kernel = functools.partial(ladder_one_kernel, groups=counts, after=len(after))
        out_shape = jax.ShapeDtypeStruct((total, width), jnp.float32)
        out_specs = pl.BlockSpec((total, tile), lambda n, at: (0, n))
    return pl.pallas_call(
        kernel,
        grid_spec=pltpu.PrefetchScalarGridSpec(
            num_scalar_prefetch=1,
            grid=(tiles,),
            in_specs=specs + [ANY] * len(after),
            out_specs=out_specs,
            scratch_shapes=scratch,
        ),
        out_shape=out_shape,
        compiler_params=params(),
        cost_estimate=light(),
    )(at, *operands, *after)


def turn_kernel(at_ref, *refs, trailer):
    for near, (base_ref, got_ref) in enumerate((refs[2:4], refs[0:2])):

        @pl.when(at_ref[0] == near)
        def _(near=near, base_ref=base_ref, got_ref=got_ref):
            put(refs[-1], [base_ref[0] + take(got_ref, 1, 0, WIDE if near else TRAILER)], trailer)


def turn(at, chunk0, chunk1, part, after=(), weight=4, trailer=TRAILER):
    _, rows, width = chunk1[0].shape
    operands, specs = [], []
    for (keep, got), index in ((chunk0, part), (chunk1, 0)):
        operands += [keep, got]
        specs.append(pl.BlockSpec((1, rows, width), lambda n, at, index=index: (0, 0, index)))
        specs.append(pl.BlockSpec((got.shape[0], width), lambda n, at, index=index: (0, index)))
    return pl.pallas_call(
        functools.partial(turn_kernel, trailer=trailer),
        grid_spec=pltpu.PrefetchScalarGridSpec(
            num_scalar_prefetch=1,
            grid=(1,),
            in_specs=specs + [ANY] * len(after),
            out_specs=pl.BlockSpec((rows + trailer, width), lambda n, at: (0, n)),
        ),
        out_shape=jax.ShapeDtypeStruct((rows + trailer, width), jnp.int16),
        compiler_params=params(),
        cost_estimate=light(weight),
    )(at, *operands, *after)


def scaled(message, side, group):
    trailer = message[2][group : group + 1, :].astype(jnp.int32).astype(jnp.float32)
    scale = jnp.exp2(trailer * (1.0 / STEPS)) * (1.0 / TOP)
    return message[side][...].astype(jnp.int32).astype(jnp.float32) * scale


class Blocks:
    def __init__(self, steps):
        self.steps, self.operands, self.specs = steps, [], []

    def add(self, array, shape, index):
        self.operands.append(array)
        self.specs.append(pl.BlockSpec(shape, index))

    def place(self, at, side, n, near):
        place = side * self.steps + n
        return place if near is None else jnp.where(at[0] == near, place, 0)

    def message(self, array, trailer, near=None):
        rows, width = (array.shape[0] - trailer) // 2 // self.steps, array.shape[1]
        for side in range(2):
            self.add(array, (rows, width), lambda n, at, *_, side=side: (self.place(at, side, n, near), 0))
        last = (array.shape[0] - trailer) // trailer
        self.add(array, (trailer, width), lambda n, *_: (last, 0))

    def sides(self, array, first, near=None):
        rows, width = array.shape[1] // 2 // self.steps, array.shape[2]
        for side in range(2):
            self.add(array, (1, rows, width), lambda n, at, *_, side=side: (first, self.place(at, side, n, near), 0))


def settle_kernel(at_ref, *refs):
    *refs, out_ref, cycle_ref, ladder_ref = refs
    near, core = at_ref[0], at_ref[1]
    refs = list(refs)

    def next_refs(count):
        return [refs.pop(0) for _ in range(count)]

    base, chain = next_refs(2), next_refs(3)
    for side in range(2):
        cycle_ref[side] = base[side][0] + scaled(chain, side, side)

    slab, occ, block, lanes = out_ref.shape
    keep0, x0 = next_refs(2), next_refs(3)
    chunk1 = [(next_refs(2), next_refs(3)) for _ in range(2)]
    came = [next_refs(3) for _ in range(2)]
    rows = keep0[0].shape[1]

    def spread(part, side, total):
        total = total + scaled(came[part], side, 0)
        for a in range(block // 2):
            row = ((part * (block // 2) + a) * 2 + side) * rows
            ladder_ref[row : row + rows, :] = total[:, a * lanes : (a + 1) * lanes]

    @pl.when(near == 1)
    def _():
        for side in range(2):
            total = keep0[side][0] + scaled(x0, side, 0)
            half = total.shape[1] // 2
            for part in range(2):
                spread(part, side, total[:, part * half : (part + 1) * half])

    @pl.when(near != 1)
    def _():
        for part, (keep, got) in enumerate(chunk1):
            for side in range(2):
                spread(part, side, keep[side][0] + scaled(got, side, 0))

    per = occ // 2

    def row(i, carry):
        for side in range(2):
            first = jnp.where(core == side, 0, rows)
            for j in range(per):
                ladder = ladder_ref[pl.ds(first + i * per + j, block, stride=2 * rows), :]
                place = pl.ds(pl.multiple_of(i * block, block), block)
                out_ref[i, side * per + j] = ladder + cycle_ref[side, place, j * lanes : (j + 1) * lanes]
        return carry

    lax.fori_loop(0, slab, row, 0)


def settle(at, shape, sums, outer, chunk0, chunk1, came, steps=4):
    slab, occ, vir, lanes = shape
    mine, wide = sums.shape[1] // 2 // steps, sums.shape[2]
    blocks = Blocks(steps)
    blocks.sides(sums, SENT)
    blocks.message(outer, WIDE)
    blocks.sides(chunk0[0], 0, 1)
    blocks.message(chunk0[1], WIDE, 1)
    for keep, got in chunk1:
        blocks.sides(keep, 0, 0)
        blocks.message(got, TRAILER, 0)
    for array in came:
        blocks.message(array, array.shape[0] - chunk0[0].shape[1])
    rows = chunk0[0].shape[1] // 2 // steps
    return pl.pallas_call(
        settle_kernel,
        grid_spec=pltpu.PrefetchScalarGridSpec(
            num_scalar_prefetch=1,
            grid=(steps,),
            in_specs=blocks.specs,
            out_specs=pl.BlockSpec((slab // steps, occ, vir, lanes), lambda n, *_: (n, 0, 0, 0)),
            scratch_shapes=[
                pltpu.VMEM((2, mine, wide), jnp.float32),
                pltpu.VMEM((2 * vir * rows, lanes), jnp.float32),
            ],
        ),
        out_shape=jax.ShapeDtypeStruct(shape, jnp.float32),
        compiler_params=params(),
        cost_estimate=light(7),
    )(at, *blocks.operands)


def finish_kernel(at_ref, slab_ref, pair_ref, base_ref, settled_ref, *refs):
    first, second = refs[0:3], refs[3:6]
    out_ref, cycle_ref = refs[6:]
    for side in range(2):
        cycle_ref[side] = scaled(first, side, side) + scaled(second, side, side)
    slab, occ, block, lanes = out_ref.shape
    per = occ // 2
    step = pl.program_id(0)

    def row(i, carry):
        energy = base_ref[...] - slab_ref[step * slab + i]
        place = pl.ds(pl.multiple_of(i * block, block), block)
        for side in range(2):
            for j in range(per):
                total = settled_ref[i, side * per + j] + cycle_ref[side, place, j * lanes : (j + 1) * lanes]
                out_ref[i, side * per + j] = total / (energy - pair_ref[side * per + j])
        return carry

    lax.fori_loop(0, slab, row, 0)


def finish(at, slab_energy, pair_energy, base, settled, cycle, steps=2):
    slab, occ, vir, lanes = settled.shape
    blocks = Blocks(steps)
    blocks.add(base, base.shape, lambda n, *_: (0, 0))
    blocks.add(settled, (slab // steps, occ, vir, lanes), lambda n, *_: (n, 0, 0, 0))
    for array, trailer in zip(cycle, (WIDE, TRAILER)):
        blocks.message(array, trailer)
    wide = cycle[0].shape[1]
    return pl.pallas_call(
        finish_kernel,
        grid_spec=pltpu.PrefetchScalarGridSpec(
            num_scalar_prefetch=3,
            grid=(steps,),
            in_specs=blocks.specs,
            out_specs=pl.BlockSpec((slab // steps, occ, vir, lanes), lambda n, *_: (n, 0, 0, 0)),
            scratch_shapes=[pltpu.VMEM((2, slab * vir // steps, wide), jnp.float32)],
        ),
        out_shape=jax.ShapeDtypeStruct(settled.shape, jnp.float32),
        compiler_params=params(),
        cost_estimate=light(),
    )(at, slab_energy, pair_energy, *blocks.operands)


def denominators(occ_energy, vir_energy, slab_index, occ_red, vir_block):
    orbital_ids = jnp.arange(occ_energy.shape[0], dtype=jnp.int32)
    chosen = slab_index[:, None] == orbital_ids[None, :]
    slab_energy = jnp.sum(jnp.where(chosen, occ_energy[None, :], jnp.float32(0.0)), axis=1)
    pair_energy = lax.dynamic_slice_in_dim(occ_energy, lax.axis_index("red") * occ_red, occ_red)
    first_virtual = lax.dynamic_slice_in_dim(vir_energy, lax.axis_index("blk") * vir_block, vir_block)
    return (
        first_virtual[None, None, :, None]
        + vir_energy[None, None, None, :]
        - slab_energy[:, None, None, None]
        - pair_energy[None, :, None, None]
    )


ORDER = ((3, 2, 1, 0), (3, 2, 0, 1), (0, 1, 3, 2), (0, 1, 2, 3))


def paired_shards(amplitudes, ladder_ints, cycle_ints, occ_energy, vir_energy, slab_index):
    slab, occ_local, vir_local, virt = amplitudes.shape
    blk, red = lax.axis_index("blk"), lax.axis_index("red")
    chip, core = blk // 2, blk % 2
    x_place = red % 2
    along_x = [(r, r ^ 1) for r in range(4)]
    along_y = [(r, r ^ 2) for r in range(4)]
    across = [(b, b ^ 1) for b in range(8)]

    def line(*hops):
        return [(2 * a + c, 2 * b + c) for a, b in hops for c in range(2)]

    inward, middle, outward = line((0, 1), (3, 2)), line((1, 2), (2, 1)), line((1, 0), (2, 3))

    def ints(*values):
        return jnp.stack([jnp.asarray(v, jnp.int32) for v in values])

    occ_red, vir_block = 2 * occ_local, vir_local // 2
    zeros = jnp.zeros((8,), jnp.int32)

    mine = amplitudes.reshape(slab, occ_local, 2, vir_block, virt)
    mine = jnp.transpose(mine, (2, 0, 3, 1, 4)).reshape(2 * slab * vir_block, occ_local * virt)
    rx = lax.ppermute(mine, "red", along_x)
    ry = lax.ppermute(mine, "red", along_y)

    own = amplitudes.reshape(slab * occ_local, vir_local * virt)
    g1 = lax.ppermute(own, "blk", line((0, 1), (1, 0), (2, 3), (3, 2)))
    g2 = lax.ppermute(own, "blk", middle)
    own_s = lax.ppermute(own, "blk", across)
    p_own = ladder_call([[own], [own_s]], ladder_ints, zeros, False)

    on_y, on_x, g1, g2 = forward(rx, ry, through=(g1, g2), after=(p_own,))
    rx2 = lax.ppermute(on_x, "red", along_x)
    ry2 = lax.ppermute(on_y, "red", along_y)
    g3 = lax.ppermute(g1, "blk", middle)
    g4 = lax.ppermute(g2, "blk", outward)
    g1_s = lax.ppermute(g1, "blk", across)
    g2_s = lax.ppermute(g2, "blk", across)
    g3_s = lax.ppermute(g3, "blk", across)
    g4_s = lax.ppermute(g4, "blk", across)
    near_x = ints(0, jnp.where(x_place == chip % 2, 0, 1), 0, 0)
    keep0, to_x = ladder_call([[g1], [g1_s]], ladder_ints, near_x, True, prior=p_own, trailer=WIDE)
    x0 = lax.ppermute(to_x, "red", along_x)

    blocks = [mine, rx, ry, ry2, rx2]
    places = jnp.array(ORDER, jnp.int32)[chip] ^ red
    at_give, at_keep = jnp.concatenate([ints(1 - core), places]), jnp.concatenate([ints(core), places])
    give_a = cycle_call(blocks, cycle_ints, at_give, 0, after=(keep0, g2_s))
    got_a = lax.ppermute(give_a, "blk", across)
    give_b = cycle_call(blocks, cycle_ints, at_give, 1, after=(give_a, g3, g4))
    got_b = lax.ppermute(give_b, "blk", across)
    sums, s0a, s1, s2 = cycle_call(blocks, cycle_ints, at_keep, 0, got_a, after=(give_b,))
    r0a = lax.ppermute(s0a, "blk", inward)
    sums, s0b, s1, s2 = cycle_call(blocks, cycle_ints, at_keep, 1, got_b, (sums, s1, s2))
    r0b = lax.ppermute(s0b, "blk", inward)
    g5 = lax.ppermute(g3, "blk", outward)

    s1, s2, g5 = gate(s1, s2, g5, after=(sums, r0a))
    to_mid = hop(sums, 0, [r0a], 0, after=(s1,))
    g5_s = lax.ppermute(g5, "blk", across)
    mid_a = lax.ppermute(to_mid, "blk", middle)
    r1 = lax.ppermute(s1, "blk", inward)
    end = jnp.where((chip == 0) | (chip == 3), 1, 0)
    stays = jnp.where(x_place == chip // 2, 0, 1)
    rest = [[g2, g4], [g2_s, g4_s], [g3, g5], [g3_s, g5_s]]
    at = ints(0, stays, end, end, end, end)
    keep1, to_x = ladder_call(rest, ladder_ints, at, True, after=(to_mid, x0), columns=2, tile=256)
    x1 = lax.ppermute(to_x, "red", along_x)
    to_mid = hop(sums, 0, [r0b], 1, after=(keep1,))
    mid_b = lax.ppermute(to_mid, "blk", middle)
    at = ints(1, stays, end, end, end, end)
    keep2, to_x = ladder_call(rest, ladder_ints, at, True, after=(to_mid,), columns=2, tile=256)
    x2 = lax.ppermute(to_x, "red", along_x)
    to_outer, s2 = hop(sums, 2, [mid_a, mid_b], parts=2, through=(s2,), after=(keep2,), weight=0, trailer=WIDE)
    r2 = lax.ppermute(s2, "blk", inward)
    outer = lax.ppermute(to_outer, "blk", outward)
    near = jnp.where(red // 2 == chip // 2, 1, 0)
    to_y1 = turn(ints(1 - near), (keep0, x0), (keep1, x1), 0, after=(to_outer,), weight=0, trailer=4 * TRAILER)
    y1 = lax.ppermute(to_y1, "red", along_y)
    to_inner = hop(sums, 1, [r1], parts=2, after=(to_y1,), weight=8)
    inner = lax.ppermute(to_inner, "blk", middle)
    to_y2 = turn(ints(1 - near), (keep0, x0), (keep2, x2), 1, after=(to_inner,), weight=0)
    y2 = lax.ppermute(to_y2, "red", along_y)

    orbital_ids = jnp.arange(occ_energy.shape[0], dtype=jnp.int32)
    chosen = slab_index[:, None] == orbital_ids[None, :]
    slab_energy = jnp.sum(jnp.where(chosen, occ_energy[None, :], jnp.float32(0.0)), axis=1)
    pair_energy = lax.dynamic_slice_in_dim(occ_energy, red * occ_red, occ_red)
    first_virtual = lax.dynamic_slice_in_dim(vir_energy, blk * vir_block, vir_block)
    base = first_virtual[:, None] + vir_energy[None, :]
    at = ints(near, core)
    shape = (slab, occ_red, vir_block, virt)
    settled = settle(at, shape, sums, outer, (keep0, x0), [(keep1, x1), (keep2, x2)], [y1, y2])
    return finish(at, slab_energy, pair_energy, base, settled, [r2, inner])


def plain_shards(amplitudes, ladder_ints, cycle_ints, occ_energy, vir_energy, slab_index):
    slab_rows, occ_local, vir_local, virt_width = amplitudes.shape
    occ_all = occ_local * lax.axis_size("blk")
    occ_red = occ_all // lax.axis_size("red")
    shard_piece = lax.all_gather(amplitudes, "blk", axis=1, tiled=True)
    row_count = shard_piece.shape[1]
    flattened = shard_piece.reshape(slab_rows * row_count, vir_local * virt_width)
    product = jnp.dot(flattened, ladder_ints, preferred_element_type=jnp.float32)
    ladder = product.reshape(slab_rows, row_count, ladder_ints.shape[1])
    ladder_own = lax.psum_scatter(ladder, "red", scatter_dimension=1, tiled=True)
    ladder_own = ladder_own.reshape(slab_rows, occ_red, -1, virt_width)
    shard_piece = lax.all_gather(amplitudes, "red", axis=2, tiled=True)
    vir_count = shard_piece.shape[2]
    operand = jnp.transpose(shard_piece, (0, 2, 1, 3)).reshape(slab_rows * vir_count, occ_local * virt_width)
    product = jnp.dot(operand, cycle_ints, preferred_element_type=jnp.float32)
    cycle_term = product.reshape(slab_rows, vir_count, cycle_ints.shape[1])
    cycle_own = lax.psum_scatter(cycle_term, "blk", scatter_dimension=1, tiled=True)
    vir_block = cycle_own.shape[1]
    cycle_own = jnp.transpose(cycle_own.reshape(slab_rows, vir_block, occ_red, virt_width), (0, 2, 1, 3))
    return (ladder_own + cycle_own) / denominators(occ_energy, vir_energy, slab_index, occ_red, vir_block)


def solution(mesh):
    placed = (P(None, "blk", "red", None), P("red", "blk"), P("blk", "red"), P(), P(), P())
    shards = paired_shards if (mesh.shape["blk"], mesh.shape["red"]) == (8, 4) else plain_shards
    return jax.shard_map(
        shards, mesh=mesh, in_specs=placed, out_specs=P(None, "red", "blk", None), check_vma=False
    )
```
